32 devices in a mesh: groups: 2 (over x), tp: 8 (over z, y), dp: 2 (over core).
Axes of the slice: x: 2, y: 2, z: 4, core: 2. Of those that a mesh axis runs over, the one named last changes fastest.
Arguments:
- queries: bfloat16 [4, 384, 8192], P(('groups', 'dp'), None, 'tp'), parts along dimension 0, may hold values from -200 to 200
- cached_key_rows: bfloat16 [4, 384, 64, 1024], P(('groups', 'dp'), 'tp'), parts along dimension 0, may hold values from -6 to 6
- cached_value_rows: bfloat16 [4, 384, 64, 1024], P(('groups', 'dp'), 'tp'), parts along dimension 0, may hold values from -6 to 6
- fresh_key_value: bfloat16 [4, 384, 2, 1024], P(('groups', 'dp'), 'tp'), parts along dimension 0, may hold values from -6 to 6
- lengths: int32 [4, 384], P(('groups', 'dp'), 'tp'), parts along dimension 0, may hold values from 2 to 64, as said below
- residual: bfloat16 [4, 384, 8192], P(('groups', 'dp'), 'tp'), parts along dimension 0, may hold values from -6 to 6
- output_weight: bfloat16 [8192, 8192], P('tp'), may hold values from -0.0625 to 0.0625
- adapter_down: bfloat16 [64, 8192, 128], P('dp', 'tp'), may hold values from -0.0625 to 0.0625
- adapter_up: bfloat16 [64, 128, 8192], P('dp', None, 'tp'), may hold values from -0.5 to 0.5
- rank: int32 [64], replicated, may hold values from 16 to 128, as said below
- requests: int32 [4, 16], P(('groups', 'dp')), parts along dimension 0, may hold values from 0 to 63, as said below
- row_choice: int32 [4, 384], P(('groups', 'dp')), parts along dimension 0, may hold values from 0 to 47
Outputs:
- block_output: bfloat16 [4, 384, 8192], P(('groups', 'dp'), 'tp'), parts along dimension 0
The draws below stay inside these ranges and needn't reach their ends.
There are 2 independent parts, one for each index of `groups`. The reference program is written for one: setup_inputs(seed, part) draws one part's arguments, and reference() takes and returns one part's arrays. A program takes and returns all parts, laid end to end along the dimension named above; an argument that names none is the same for every part. Nothing has to cross between parts.
Inputs may be any that keep to these rules, and one draw needn't show every extreme that they name: `lengths`: every length from 2 to 64 occurs. `rank`: a multiple of 16; each such multiple occurs. `requests`: the list of data index p names 16 different pool slots, none owned by p; slot s is owned by data index s // 32.
All inputs are finite; a program needn't handle non-finite values.
Results may differ from the reference program's by a relative error of at most 0.008.
Values may be sent and summed in bfloat16 or wider, within the bound.
No kernel may reach another device: no remote copies, remote signals or barrier semaphores. Data moves between devices by JAX's collectives and lax.ppermute only.
A program may use at most 192 MiB of HBM per device.

```python
import math
import jax
import jax.numpy as jnp
import numpy as np
from jax import lax

MODEL_WIDTH = 8192
HEADS = 64
KV_HEADS = 8
HEAD_DIM = 128
PADDED_RANK = 128
LEN = 64
ADP_DEV = 32
FETCH = 16
ROWS_DP = 384
ADAPTER_POOL = 64
N_TP = 8
N_DP = 2


def first_keys(key):
    anchor = jax.random.normal(jax.random.fold_in(key, 11), (N_DP, ROWS_DP, KV_HEADS * HEAD_DIM), jnp.float32)
    return jnp.clip(anchor, -6.0, 6.0)


def draw_cached_key_rows(key, part):
    anchor = first_keys(key)
    key = jax.random.fold_in(key, 1)
    array_shape = (N_DP, ROWS_DP, LEN, KV_HEADS * HEAD_DIM)
    values = jnp.clip(jax.random.normal(key, array_shape, jnp.float32), -6.0, 6.0)
    values = values.at[:, :, 0].set(anchor)
    return values.astype(jnp.bfloat16)


def draw_queries(key, part):
    key = jax.random.fold_in(key, 2)
    array_shape = (N_DP, ROWS_DP, HEADS * HEAD_DIM)
    values = jnp.clip(jax.random.normal(key, array_shape, jnp.float32), -6.0, 6.0)
    return values.astype(jnp.bfloat16)


def draw_lengths(key, part):
    key = jax.random.fold_in(key, 3)
    sort_order = jax.random.permutation(key, N_DP * ROWS_DP).astype(jnp.int32)
    return (2 + sort_order % (LEN - 1)).reshape(N_DP, ROWS_DP).astype(jnp.int32)


def draw_rank(key, part):
    key = jax.random.fold_in(key, 4)
    sort_order = jax.random.permutation(key, ADAPTER_POOL).astype(jnp.int32)
    return (PADDED_RANK // 8 * (1 + sort_order % 8)).astype(jnp.int32)


def draw_requests(key, part):
    key = jax.random.fold_in(key, 5)
    foreign = (N_DP - 1) * ADP_DEV
    reader = jnp.arange(N_DP, dtype=jnp.int32)[:, None]
    position = jnp.arange(foreign, dtype=jnp.int32)[None, :]
    noise = jax.random.randint(key, (N_DP, foreign), 0, 4096, jnp.int32)
    score_table = noise * foreign + position
    extreme = jnp.where(reader == 0, foreign - 1, 0)
    score_table = jnp.where(position == extreme, -1, score_table)
    chosen = jnp.argsort(score_table, axis=1)[:, :FETCH].astype(jnp.int32)
    slot_table = jnp.where(chosen < reader * ADP_DEV, chosen, chosen + ADP_DEV)
    return slot_table.astype(jnp.int32)


def touch_ends(result, rng, smallest, high):
    extent = result.shape
    index_at = [jax.random.randint(jax.random.fold_in(rng, axis), (), 0, extent[axis]) for axis in range(len(extent))]
    result = result.at[tuple(index_at)].set(smallest)
    longest = extent.index(max(extent))
    index_at[longest] = (index_at[longest] + 1) % extent[longest]
    return result.at[tuple(index_at)].set(high)


def block_scale(rng, shape, split, smallest, high):
    def one(dim, parts):
        steps = jax.random.uniform(jax.random.fold_in(jax.random.fold_in(rng, 6), dim), (parts,), jnp.float32, smallest / len(split), high / len(split))
        return jnp.repeat(jnp.exp(steps), shape[dim] // parts).reshape((-1,) + (1,) * (len(shape) - dim - 1))

    level = one(*split[0])
    for cut in split[1:]:
        level = level * one(*cut)
    return level


def rank_table(count, lean):
    portions = [(1 << 20) // math.isqrt(grade ** lean) + 1 for grade in range(1, count + 1)]
    deviation = 1 + sum(portions) // (1 << 30)
    return np.cumsum(np.array([max(1, weight // deviation) for weight in portions]))


def skewed_ids(own_key, dims, amount, skew):
    listing = rank_table(amount, skew)
    lot = jax.random.randint(jax.random.fold_in(own_key, 1), dims, 0, int(listing[amount - 1]))
    grade = jnp.searchsorted(jnp.asarray(listing, jnp.int32), lot, side="right")
    return jax.random.permutation(jax.random.fold_in(own_key, 2), amount)[grade].astype(jnp.int32)


def bell_draw(key, extent, deviation, limit, pieces=(), held_as=jnp.bfloat16):
    array = jax.random.normal(key, extent, jnp.float32) * deviation
    if len(pieces) > 0:
        array = block_scale(key, extent, pieces, -0.22, 0.18) * array
    return jnp.clip(array, min=-limit, max=limit).astype(held_as)


def setup_inputs(seed: int = 0, part: int = 0) -> dict:
    key_of = jax.random.split(jax.random.key(seed), 13)
    part_splits = jax.random.split(jax.random.fold_in(key_of[12], part), 13)
    return {
        "queries": draw_queries(jax.random.fold_in(jax.random.fold_in(key_of[12], part), 71), part),
        "cached_key_rows": draw_cached_key_rows(jax.random.fold_in(jax.random.fold_in(key_of[12], part), 71), part),
        "cached_value_rows": bell_draw(part_splits[2], (N_DP, ROWS_DP, LEN, KV_HEADS * HEAD_DIM), 1.0, 6.0, ((0, 2), (1, 8))),
        "fresh_key_value": bell_draw(part_splits[3], (N_DP, ROWS_DP, 2, KV_HEADS * HEAD_DIM), 1.0, 6.0, ((0, 2), (1, 8))),
        "lengths": draw_lengths(jax.random.fold_in(jax.random.fold_in(key_of[12], part), 71), part),
        "residual": bell_draw(part_splits[5], (N_DP, ROWS_DP, MODEL_WIDTH), 1.0, 6.0, ((0, 2), (1, 8))),
        "output_weight": bell_draw(key_of[6], (MODEL_WIDTH, MODEL_WIDTH), MODEL_WIDTH ** -0.5, 0.0625, ((0, 8),)),
        "adapter_down": bell_draw(key_of[7], (ADAPTER_POOL, MODEL_WIDTH, PADDED_RANK), MODEL_WIDTH ** -0.5, 0.0625, ((0, 2), (1, 8))),
        "adapter_up": bell_draw(key_of[8], (ADAPTER_POOL, PADDED_RANK, MODEL_WIDTH), PADDED_RANK ** -0.5, 0.5, ((0, 2), (2, 8))),
        "rank": draw_rank(jax.random.fold_in(key_of[12], 71), part),
        "requests": draw_requests(jax.random.fold_in(jax.random.fold_in(key_of[12], part), 71), part),
        "row_choice": touch_ends(skewed_ids(part_splits[11], (N_DP, ROWS_DP), ADP_DEV + FETCH, 2), jax.random.fold_in(part_splits[11], 3), 0, (ADP_DEV + FETCH) - 1).astype(jnp.int32),
    }


ADAPTER_SCALE = 0.25


def attend(query_rows, key_cache, value_cache, new_entries, lengths):
    row_count = query_rows.shape[0]
    positions = key_cache.shape[1]
    groups = HEADS // KV_HEADS
    scale_factor = HEAD_DIM ** -0.5
    query_grid = query_rows.astype(jnp.float32).reshape(row_count, KV_HEADS, groups, HEAD_DIM)
    key_grid = key_cache.astype(jnp.float32).reshape(row_count, positions, KV_HEADS, HEAD_DIM)
    value_grid = value_cache.astype(jnp.float32).reshape(row_count, positions, KV_HEADS, HEAD_DIM)
    new_key = new_entries[:, 0].astype(jnp.float32).reshape(row_count, KV_HEADS, HEAD_DIM)
    new_value = new_entries[:, 1].astype(jnp.float32).reshape(row_count, KV_HEADS, HEAD_DIM)
    scores = jnp.einsum("rkgd,rjkd->rkgj", query_grid, key_grid) * scale_factor
    live_mask = jnp.arange(positions)[None, :] < lengths[:, None]
    scores = jnp.where(live_mask[:, None, None, :], scores, -jnp.inf)
    own_score = jnp.einsum("rkgd,rkd->rkg", query_grid, new_key) * scale_factor
    peak_score = jnp.maximum(jnp.max(scores, axis=3), own_score)
    weights = jnp.exp(scores - peak_score[..., None])
    own_weight = jnp.exp(own_score - peak_score)
    weight_sum = jnp.sum(weights, axis=3) + own_weight
    prob_cache = (weights / weight_sum[..., None]).astype(jnp.bfloat16)
    prob_new = (own_weight / weight_sum).astype(jnp.bfloat16)
    attended = jnp.einsum("rkgj,rjkd->rkgd", prob_cache.astype(jnp.float32), value_grid)
    attended = attended + prob_new.astype(jnp.float32)[..., None] * new_value[:, :, None, :]
    return attended.reshape(row_count, HEADS * HEAD_DIM).astype(jnp.bfloat16)


def reference(queries, cached_key_rows, cached_value_rows, fresh_key_value, lengths, residual, output_weight, adapter_down, adapter_up, rank, requests, row_choice):
    row_count = N_DP * ROWS_DP
    kv_width = KV_HEADS * HEAD_DIM
    attention_output = attend(queries.reshape(row_count, MODEL_WIDTH), cached_key_rows.reshape(row_count, LEN, kv_width), cached_value_rows.reshape(row_count, LEN, kv_width), fresh_key_value.reshape(row_count, 2, kv_width), lengths.reshape(row_count))
    block_of = (jnp.arange(row_count) // ROWS_DP).astype(jnp.int32)
    row_picks = row_choice.reshape(row_count).astype(jnp.int32)
    fetched_slot = requests[block_of, jnp.clip(row_picks - ADP_DEV, 0, FETCH - 1).astype(jnp.int32)]
    slots_of_rows = jnp.where(row_picks < ADP_DEV, block_of * ADP_DEV + row_picks, fetched_slot).astype(jnp.int32)
    rank_of_row = rank[slots_of_rows]

    def row_inner(packed_row):
        vector, slot_number = packed_row
        down_factor = lax.dynamic_index_in_dim(adapter_down, slot_number, 0, keepdims=False)
        return jnp.dot(vector, down_factor, preferred_element_type=jnp.float32)

    adapter_inner = lax.map(row_inner, (attention_output, slots_of_rows))
    mask_of_rank = jnp.arange(PADDED_RANK)[None, :] < rank_of_row[:, None]
    row_factor = ADAPTER_SCALE * PADDED_RANK / rank_of_row.astype(jnp.float32)
    scaled_output = jnp.where(mask_of_rank, adapter_inner * row_factor[:, None], 0.0).astype(jnp.bfloat16)

    def row_outer(packed_row):
        vector, slot_number = packed_row
        up_factor = lax.dynamic_index_in_dim(adapter_up, slot_number, 0, keepdims=False)
        return jnp.dot(vector, up_factor, preferred_element_type=jnp.float32)

    adapter_delta = lax.map(row_outer, (scaled_output, slots_of_rows))
    head_column_span = MODEL_WIDTH // N_TP

    def add_shard(running, shard_index):
        column_start = shard_index * head_column_span
        part_attention = lax.dynamic_slice_in_dim(attention_output, column_start, head_column_span, 1)
        part_weight = lax.dynamic_slice_in_dim(output_weight, column_start, head_column_span, 0)
        summed_shard = jnp.dot(part_attention, part_weight, preferred_element_type=jnp.float32)
        owned_columns = lax.dynamic_slice_in_dim(summed_shard, column_start, head_column_span, 1) + lax.dynamic_slice_in_dim(adapter_delta, column_start, head_column_span, 1)
        summed_shard = lax.dynamic_update_slice_in_dim(summed_shard, owned_columns, column_start, 1)
        rounded = lax.optimization_barrier(summed_shard.astype(jnp.bfloat16))
        return running + rounded.astype(jnp.float32), None

    summed, _ = lax.scan(add_shard, jnp.zeros((row_count, MODEL_WIDTH), jnp.float32), jnp.arange(N_TP, dtype=jnp.int32))
    block_output = (residual.reshape(row_count, MODEL_WIDTH).astype(jnp.float32) + summed).astype(jnp.bfloat16)
    return block_output.reshape(N_DP, ROWS_DP, MODEL_WIDTH)
```

```python
import functools

import jax
import jax.numpy as jnp
from jax import lax
from jax.experimental import pallas as pl
from jax.experimental.pallas import tpu as pltpu
from jax.sharding import PartitionSpec as P

HEADS = 64
KV_HEADS = 8
HEAD_DIM = 128
ADAPTER_SCALE = 0.25
BF16 = jnp.bfloat16
F32 = jnp.float32
ROW_BLOCK = 16
SUB = 8
VMEM_LIMIT = 48 * 1024 * 1024


def permute_xor(x, axis, size, k):
    return lax.ppermute(x, axis, [(i, i ^ k) for i in range(size)])


def attend_kernel(n, me_ref, q_ref, k_ref, v_ref, fk_ref, fv_ref, len_ref, o_ref):
    me = me_ref[0]
    groups = HEADS // KV_HEADS
    per_src = HEADS // n
    positions = k_ref.shape[1]
    lanes = 2 * positions
    tiles = SUB // 2
    rows = groups * SUB
    row_of = lax.broadcasted_iota(jnp.int32, (rows, lanes), 0) % SUB
    lane_of = lax.broadcasted_iota(jnp.int32, (rows, lanes), 1)
    in_row = (row_of % 2) == (lane_of // positions)
    tile_of = row_of // 2
    scale = HEAD_DIM ** (-0.5)
    for c in range(KV_HEADS):
        span = slice(c * HEAD_DIM, (c + 1) * HEAD_DIM)
        heads = [c * groups + h for h in range(groups)]
        q_heads = [
            q_ref[(h // per_src) ^ me, :, (h % per_src) * HEAD_DIM : (h % per_src + 1) * HEAD_DIM].astype(F32)
            for h in heads
        ]
        outs = []
        for s in range(ROW_BLOCK // SUB):
            part = slice(s * SUB, (s + 1) * SUB)
            q_f32 = jnp.concatenate([q[part] for q in q_heads], axis=0)
            keys = k_ref[part, :, span].reshape(SUB * positions, HEAD_DIM)
            values = v_ref[part, :, span].reshape(SUB * positions, HEAD_DIM)
            full = lax.dot_general(
                q_f32.astype(BF16), keys, (((1,), (1,)), ((), ())), preferred_element_type=F32
            )
            score = full[:, :lanes]
            for k in range(1, tiles):
                score = jnp.where(tile_of == k, full[:, k * lanes : (k + 1) * lanes], score)
            live = in_row & ((lane_of % positions) < jnp.tile(len_ref[part], (groups, 1)))
            score = jnp.where(live, score * scale, -1e30)
            fresh_key = jnp.tile(fk_ref[:, span].astype(F32)[part], (groups, 1))
            fresh_value = jnp.tile(fv_ref[:, span].astype(F32)[part], (groups, 1))
            own = jnp.sum(q_f32 * fresh_key, axis=1, keepdims=True) * scale
            peak = jnp.maximum(jnp.max(score, axis=1, keepdims=True), own)
            weight = jnp.where(live, jnp.exp(score - peak), 0.0)
            own_weight = jnp.exp(own - peak)
            total = jnp.sum(weight, axis=1, keepdims=True) + own_weight
            prob = weight / total
            prob_new = (own_weight / total).astype(BF16).astype(F32)
            wide = jnp.concatenate([jnp.where(tile_of == k, prob, 0.0) for k in range(tiles)], axis=1).astype(BF16)
            outs.append(jnp.dot(wide, values, preferred_element_type=F32) + prob_new * fresh_value)
        for i, h in enumerate(heads):
            block = jnp.concatenate([o[i * SUB : (i + 1) * SUB] for o in outs], axis=0).astype(BF16)
            o_ref[(h // per_src) ^ me, :, (h % per_src) * HEAD_DIM : (h % per_src + 1) * HEAD_DIM] = block


def attend(me, q, keys, values, fresh_key, fresh_value, lengths):
    n, rows, width = q.shape
    kv = keys.shape[2]
    positions = keys.shape[1]
    return pl.pallas_call(
        functools.partial(attend_kernel, n),
        grid_spec=pltpu.PrefetchScalarGridSpec(
            num_scalar_prefetch=1,
            grid=(rows // ROW_BLOCK,),
            in_specs=[
                pl.BlockSpec((n, ROW_BLOCK, width), lambda i, me: (0, i, 0)),
                pl.BlockSpec((ROW_BLOCK, positions, kv), lambda i, me: (i, 0, 0)),
                pl.BlockSpec((ROW_BLOCK, positions, kv), lambda i, me: (i, 0, 0)),
                pl.BlockSpec((ROW_BLOCK, kv), lambda i, me: (i, 0)),
                pl.BlockSpec((ROW_BLOCK, kv), lambda i, me: (i, 0)),
                pl.BlockSpec((ROW_BLOCK, 1), lambda i, me: (i, 0)),
            ],
            out_specs=pl.BlockSpec((n, ROW_BLOCK, width), lambda i, me: (0, i, 0)),
        ),
        out_shape=jax.ShapeDtypeStruct((n, rows, width), BF16),
        compiler_params=pltpu.CompilerParams(vmem_limit_bytes=VMEM_LIMIT),
        cost_estimate=pl.CostEstimate(
            flops=4 * rows * SUB * HEADS * HEAD_DIM * positions,
            bytes_accessed=4 * rows * positions * kv,
            transcendentals=rows * HEADS * positions,
        ),
        name="attend",
    )(me, q, keys, values, fresh_key, fresh_value, lengths)


def inner_kernel(per, a_ref, b_ref, ia_ref, ib_ref, down_ref, oa_ref, ob_ref, acc_a, acc_b):
    step = pl.program_id(0)

    @pl.when(step == 0)
    def _():
        acc_a[...] = jnp.zeros_like(acc_a)
        acc_b[...] = jnp.zeros_like(acc_b)

    rank = down_ref.shape[2]
    wide = jnp.concatenate([down_ref[i] for i in range(per)], axis=1)
    for x_ref, id_ref, acc in ((a_ref, ia_ref, acc_a), (b_ref, ib_ref, acc_b)):
        product = jnp.dot(x_ref[...], wide, preferred_element_type=F32)
        total = acc[...]
        for i in range(per):
            total = jnp.where(id_ref[...] == step * per + i, product[:, i * rank : (i + 1) * rank], total)
        acc[...] = total

    @pl.when(step == pl.num_programs(0) - 1)
    def _():
        oa_ref[...] = acc_a[...].astype(BF16)
        ob_ref[...] = acc_b[...].astype(BF16)


def inner_products(rows_a, rows_b, ids_a, ids_b, down):
    rows, width = rows_a.shape
    owned, _, rank = down.shape
    per = 2
    whole = lambda shape: pl.BlockSpec(shape, lambda i: (0, 0))
    return pl.pallas_call(
        functools.partial(inner_kernel, per),
        grid=(owned // per,),
        in_specs=[
            whole((rows, width)),
            whole((rows, width)),
            whole((rows, 1)),
            whole((rows, 1)),
            pl.BlockSpec((per, width, rank), lambda i: (i, 0, 0)),
        ],
        out_specs=[whole((rows, rank)), whole((rows, rank))],
        out_shape=[jax.ShapeDtypeStruct((rows, rank), BF16)] * 2,
        scratch_shapes=[pltpu.VMEM((rows, rank), F32)] * 2,
        compiler_params=pltpu.CompilerParams(vmem_limit_bytes=VMEM_LIMIT),
        cost_estimate=pl.CostEstimate(
            flops=4 * rows * width * rank * owned, bytes_accessed=2 * owned * width * rank, transcendentals=0
        ),
        name="inner_products",
    )(rows_a, rows_b, ids_a, ids_b, down)


def delta_kernel(per, a_ref, b_ref, ia_ref, ib_ref, up_ref, oa_ref, ob_ref, acc_a, acc_b):
    step = pl.program_id(0)

    @pl.when(step == 0)
    def _():
        acc_a[...] = jnp.zeros_like(acc_a)
        acc_b[...] = jnp.zeros_like(acc_b)

    rank, width = up_ref.shape[1:]
    up = up_ref[...].reshape(per * rank, width)
    for x_ref, id_ref, acc in ((a_ref, ia_ref, acc_a), (b_ref, ib_ref, acc_b)):
        x = x_ref[...]
        ids = id_ref[...]
        wide = jnp.concatenate(
            [jnp.where(ids == step * per + i, x, jnp.zeros_like(x)) for i in range(per)], axis=1
        ).astype(BF16)
        acc[...] += jnp.dot(wide, up, preferred_element_type=F32)

    @pl.when(step == pl.num_programs(0) - 1)
    def _():
        oa_ref[...] = acc_a[...].astype(BF16)
        ob_ref[...] = acc_b[...].astype(BF16)


def adapter_outputs(scaled_a, scaled_b, ids_a, ids_b, up):
    rows, rank = scaled_a.shape
    owned, _, width = up.shape
    per = 8
    whole = lambda shape: pl.BlockSpec(shape, lambda i: (0, 0))
    return pl.pallas_call(
        functools.partial(delta_kernel, per),
        grid=(owned // per,),
        in_specs=[
            whole((rows, rank)),
            whole((rows, rank)),
            whole((rows, 1)),
            whole((rows, 1)),
            pl.BlockSpec((per, rank, width), lambda i: (i, 0, 0)),
        ],
        out_specs=[whole((rows, width)), whole((rows, width))],
        out_shape=[jax.ShapeDtypeStruct((rows, width), BF16)] * 2,
        scratch_shapes=[pltpu.VMEM((rows, width), F32)] * 2,
        compiler_params=pltpu.CompilerParams(vmem_limit_bytes=VMEM_LIMIT),
        cost_estimate=pl.CostEstimate(
            flops=4 * rows * width * rank * owned, bytes_accessed=2 * owned * width * rank, transcendentals=0
        ),
        name="adapter_outputs",
    )(scaled_a, scaled_b, ids_a, ids_b, up)


def project_kernel(with_delta, half, where_ref, x_ref, w_ref, *refs):
    if with_delta:
        d_ref, near_ref, far_ref = refs
    else:
        near_ref, far_ref = refs
    result = jnp.dot(x_ref[...], w_ref[...], preferred_element_type=F32)
    if with_delta:
        result = result + jnp.where(where_ref[1] == 1, d_ref[...].astype(F32), 0.0)
    near_ref[...] = result[:half].astype(BF16)
    far_ref[...] = result[half:].astype(BF16)


def project(where, x, weight, width, delta=None):
    rows, depth = x.shape
    half = rows // 2
    tile = min(256, width)
    per = width // tile
    ins = [
        pl.BlockSpec((rows, depth), lambda i, w: (0, 0)),
        pl.BlockSpec((depth, tile), lambda i, w: (0, w[0] * per + i)),
    ]
    args = [x, weight]
    if delta is not None:
        ins.append(pl.BlockSpec((rows, tile), lambda i, w: (0, i)))
        args.append(delta)
    return pl.pallas_call(
        functools.partial(project_kernel, delta is not None, half),
        grid_spec=pltpu.PrefetchScalarGridSpec(
            num_scalar_prefetch=1,
            grid=(per,),
            in_specs=ins,
            out_specs=[pl.BlockSpec((half, tile), lambda i, w: (0, i))] * 2,
        ),
        out_shape=[jax.ShapeDtypeStruct((half, width), BF16)] * 2,
        compiler_params=pltpu.CompilerParams(vmem_limit_bytes=VMEM_LIMIT),
        cost_estimate=pl.CostEstimate(
            flops=2 * rows * depth * width, bytes_accessed=2 * depth * width, transcendentals=0
        ),
        name="project",
    )(where, *args)


def finish_kernel(terms, width, order_ref, res_ref, *refs):
    o_ref = refs[-1]
    count = (len(refs) - 1) // terms
    for i in range(count):
        place = pl.ds(pl.multiple_of(order_ref[i] * width, width), width)
        total = refs[i * terms][...].astype(F32)
        for j in range(1, terms):
            total = total + refs[i * terms + j][...].astype(F32)
        o_ref[:, place] = (res_ref[:, place].astype(F32) + total).astype(BF16)


def finish(order, residual, columns):
    rows, features = residual.shape
    terms = len(columns[0])
    width = columns[0][0].shape[1]
    flat = [x for group in columns for x in group]
    vmem = pl.BlockSpec(memory_space=pltpu.VMEM)
    return pl.pallas_call(
        functools.partial(finish_kernel, terms, width),
        in_specs=[pl.BlockSpec(memory_space=pltpu.SMEM), vmem] + [vmem] * len(flat),
        out_specs=vmem,
        out_shape=jax.ShapeDtypeStruct((rows, features), BF16),
        compiler_params=pltpu.CompilerParams(vmem_limit_bytes=VMEM_LIMIT),
        cost_estimate=pl.CostEstimate(
            flops=terms * rows * features, bytes_accessed=2 * (terms + 2) * rows * features, transcendentals=0
        ),
        name="finish",
    )(order, residual, *flat)


def shards(
    n,
    n_dp,
    queries,
    cached_key_rows,
    cached_value_rows,
    fresh_key_value,
    lengths,
    residual,
    output_weight,
    adapter_down,
    adapter_up,
    rank,
    requests,
    row_choice,
):
    nz = n // 2
    me = lax.axis_index("tp").astype(jnp.int32)
    dp = lax.axis_index("dp").astype(jnp.int32)
    z, y = me // 2, me % 2
    rows_dp = queries.shape[1]
    rows = rows_dp // n
    width = queries.shape[2]
    pool_rank = adapter_down.shape[2]
    owned = adapter_down.shape[0]
    fetch = requests.shape[1]
    order = [k for k in range(n) if k % 2 == 0] + [k for k in range(n) if k % 2 == 1]

    q_blocks = queries[0].reshape(n, rows, width)
    q_parts = []
    for k in range(n):
        block = lax.dynamic_index_in_dim(q_blocks, me ^ k, 0, keepdims=False)
        q_parts.append(block if k == 0 else permute_xor(block, "tp", n, k))
    q = jnp.stack(q_parts)
    attended = attend(
        me[None],
        q,
        cached_key_rows[0],
        cached_value_rows[0],
        fresh_key_value[0, :, 0],
        fresh_key_value[0, :, 1],
        lengths[0][:, None],
    )

    choice = row_choice[0].reshape(n, rows)
    choice = jnp.concatenate([lax.dynamic_index_in_dim(choice, me ^ k, 0, keepdims=False) for k in order])
    lists = requests[0]
    sides = []
    for side in range(2):
        if side == 1:
            choice = permute_xor(choice, "dp", n_dp, 1)
            lists = permute_xor(lists, "dp", n_dp, 1)
        hit = choice[:, None] - owned == jnp.arange(fetch, dtype=jnp.int32)[None, :]
        fetched = jnp.sum(jnp.where(hit, lists[None, :], 0), axis=1)
        slot = jnp.where(choice < owned, (dp ^ side) * owned + choice, fetched)
        local = slot - dp * owned
        mine = (local >= 0) & (local < owned)
        pool = jnp.arange(rank.shape[0], dtype=jnp.int32)
        row_rank = jnp.sum(jnp.where(slot[:, None] == pool[None, :], rank[None, :], 0), axis=1)
        factor = jnp.where(
            (jnp.arange(pool_rank)[None, :] < row_rank[:, None]) & mine[:, None],
            (ADAPTER_SCALE * pool_rank / row_rank.astype(F32))[:, None],
            0.0,
        )
        sides.append((local[:, None], factor))
    (ids_a, factor_a), (ids_b, factor_b) = sides

    x = jnp.concatenate(
        [attended[0] if k == 0 else permute_xor(attended[k], "tp", n, k) for k in order], axis=0
    )
    x_other = permute_xor(x, "dp", n_dp, 1)

    inner_a, inner_b = inner_products(x, x_other, ids_a, ids_b, adapter_down)
    inner = inner_a.astype(F32) + permute_xor(inner_b, "dp", n_dp, 1).astype(F32)
    step = 1
    while step < n:
        part = permute_xor(inner.astype(BF16), "tp", n, step).reshape(n, rows, pool_rank)
        part = jnp.concatenate([part[order.index(k ^ step)] for k in order], axis=0)
        inner = inner + part.astype(F32)
        step *= 2
    inner_other = permute_xor(inner.astype(BF16), "dp", n_dp, 1).astype(F32)
    delta_a, delta_b = adapter_outputs(
        (inner * factor_a).astype(BF16), (inner_other * factor_b).astype(BF16), ids_a, ids_b, adapter_up
    )
    delta = (delta_a.astype(F32) + permute_xor(delta_b, "dp", n_dp, 1).astype(F32)).astype(BF16)

    mine_sums, received = {}, {}
    for jz in reversed(range(nz)):
        for b in range(2):
            place = (z ^ jz) * 2 + b
            flag = (y == b).astype(jnp.int32)
            near, far = project(
                jnp.stack([place, flag]), x, output_weight, width, delta if jz == 0 else None
            )
            far = permute_xor(far, "tp", n, 1)
            total = (near.astype(F32) + far.astype(F32)).astype(BF16).reshape(nz, rows, width)
            mine_sums[jz, b] = total[0]
            for j in range(1, nz):
                received[j, jz, b] = permute_xor(total[j], "tp", n, 2 * j)
    columns, places = [], []
    for jz in range(nz):
        for b in range(2):
            places.append((z ^ jz) * 2 + b)
            columns.append([mine_sums[jz, b]] + [received[j, jz ^ j, b] for j in range(1, nz)])
    return finish(jnp.stack(places), residual[0], columns)[None]


def solution(mesh):
    return jax.shard_map(
        functools.partial(shards, mesh.shape["tp"], mesh.shape["dp"]),
        mesh=mesh,
        in_specs=(
            P(("groups", "dp"), None, "tp"),
            P(("groups", "dp"), "tp", None, None),
            P(("groups", "dp"), "tp", None, None),
            P(("groups", "dp"), "tp", None, None),
            P(("groups", "dp"), "tp"),
            P(("groups", "dp"), "tp", None),
            P("tp", None),
            P("dp", "tp", None),
            P("dp", None, "tp"),
            P(),
            P(("groups", "dp"), None),
            P(("groups", "dp"), None),
        ),
        out_specs=P(("groups", "dp"), "tp", None),
        check_vma=False,
    )
```

```python
import functools

import jax
import jax.numpy as jnp
from jax import lax
from jax.experimental import pallas as pl
from jax.experimental.pallas import tpu as pltpu
from jax.sharding import PartitionSpec as P

HEADS = 64
KV_HEADS = 8
HEAD_DIM = 128
ADAPTER_SCALE = 0.25
BF16 = jnp.bfloat16
F32 = jnp.float32
ROW_BLOCK = 16
SUB = 8
BATCH = 4
VMEM_LIMIT = 48 * 1024 * 1024


ADD_US = 8.7


def cost(us):
    return pl.CostEstimate(flops=int(us * 1.15e9), bytes_accessed=1, transcendentals=0)


def permute_xor(x, axis, size, k):
    return lax.ppermute(x, axis, [(i, i ^ k) for i in range(size)])


def attend_kernel(n, q_ref, k_ref, v_ref, fk_ref, fv_ref, len_ref, o_ref):
    groups = HEADS // KV_HEADS
    per_src = HEADS // n
    positions = k_ref.shape[1]
    lanes = 2 * positions
    tiles = SUB // 2
    rows = groups * SUB
    row_of = lax.broadcasted_iota(jnp.int32, (rows, lanes), 0) % SUB
    lane_of = lax.broadcasted_iota(jnp.int32, (rows, lanes), 1)
    in_row = (row_of % 2) == (lane_of // positions)
    tile_of = row_of // 2
    scale = HEAD_DIM ** (-0.5)
    parts = [slice(s * SUB, (s + 1) * SUB) for s in range(ROW_BLOCK // SUB)]
    lives = [
        in_row & ((lane_of % positions) < jnp.tile(len_ref[part], (groups, 1))) for part in parts
    ]
    for first in range(0, KV_HEADS, BATCH):
        batch = range(first, first + BATCH)
        scores, owns, values, fresh = [], [], [], []
        for c in batch:
            span = slice(c * HEAD_DIM, (c + 1) * HEAD_DIM)
            heads = [c * groups + h for h in range(groups)]
            q_heads = [
                q_ref[h // per_src, :, (h % per_src) * HEAD_DIM : (h % per_src + 1) * HEAD_DIM].astype(F32)
                for h in heads
            ]
            fresh_key = fk_ref[:, span].astype(F32)
            fresh_value = fv_ref[:, span].astype(F32)
            for part, live in zip(parts, lives):
                q_f32 = jnp.concatenate([q[part] for q in q_heads], axis=0)
                keys = k_ref[part, :, span].reshape(SUB * positions, HEAD_DIM)
                full = lax.dot_general(
                    q_f32.astype(BF16), keys, (((1,), (1,)), ((), ())), preferred_element_type=F32
                )
                score = full[:, :lanes]
                for k in range(1, tiles):
                    score = jnp.where(tile_of == k, full[:, k * lanes : (k + 1) * lanes], score)
                scores.append(jnp.where(live, score * scale, -1e30))
                owns.append(
                    jnp.sum(q_f32 * jnp.tile(fresh_key[part], (groups, 1)), axis=1, keepdims=True) * scale
                )
                fresh.append(jnp.tile(fresh_value[part], (groups, 1)))
                values.append(v_ref[part, :, span].reshape(SUB * positions, HEAD_DIM))
        peaks = [jnp.maximum(jnp.max(s, axis=1, keepdims=True), o) for s, o in zip(scores, owns)]
        weights = [
            jnp.where(live, jnp.exp(s - p), 0.0) for s, p, live in zip(scores, peaks, lives * BATCH)
        ]
        own_weights = [jnp.exp(o - p) for o, p in zip(owns, peaks)]
        totals = [jnp.sum(w, axis=1, keepdims=True) + o for w, o in zip(weights, own_weights)]
        outs = []
        for w, o, t, v, f in zip(weights, own_weights, totals, values, fresh):
            prob = w / t
            prob_new = (o / t).astype(BF16).astype(F32)
            wide = jnp.concatenate([jnp.where(tile_of == k, prob, 0.0) for k in range(tiles)], axis=1)
            outs.append(jnp.dot(wide.astype(BF16), v, preferred_element_type=F32) + prob_new * f)
        for i, c in enumerate(batch):
            pair = outs[i * len(parts) : (i + 1) * len(parts)]
            for g in range(groups):
                h = c * groups + g
                block = jnp.concatenate([o[g * SUB : (g + 1) * SUB] for o in pair], axis=0).astype(BF16)
                o_ref[h // per_src, :, (h % per_src) * HEAD_DIM : (h % per_src + 1) * HEAD_DIM] = block


def attend(q, keys, values, fresh_key, fresh_value, lengths):
    n, rows, width = q.shape
    kv = keys.shape[2]
    positions = keys.shape[1]
    return pl.pallas_call(
        functools.partial(attend_kernel, n),
        grid=(rows // ROW_BLOCK,),
        in_specs=[
            pl.BlockSpec((n, ROW_BLOCK, width), lambda i: (0, i, 0)),
            pl.BlockSpec((ROW_BLOCK, positions, kv), lambda i: (i, 0, 0)),
            pl.BlockSpec((ROW_BLOCK, positions, kv), lambda i: (i, 0, 0)),
            pl.BlockSpec((ROW_BLOCK, kv), lambda i: (i, 0)),
            pl.BlockSpec((ROW_BLOCK, kv), lambda i: (i, 0)),
            pl.BlockSpec((ROW_BLOCK, 1), lambda i: (i, 0)),
        ],
        out_specs=pl.BlockSpec((n, ROW_BLOCK, width), lambda i: (0, i, 0)),
        out_shape=jax.ShapeDtypeStruct((n, rows, width), BF16),
        compiler_params=pltpu.CompilerParams(vmem_limit_bytes=VMEM_LIMIT),
        cost_estimate=cost(9),
        name="attend",
    )(q, keys, values, fresh_key, fresh_value, lengths)


def inner_kernel(per, a_ref, b_ref, ia_ref, ib_ref, down_ref, *refs):
    oa_ref, ob_ref, acc_a, acc_b = refs[-4:]
    step = pl.program_id(0)

    @pl.when(step == 0)
    def _():
        acc_a[...] = jnp.zeros_like(acc_a)
        acc_b[...] = jnp.zeros_like(acc_b)

    rank = down_ref.shape[2]
    for p in range(0, per, 2):
        wide = jnp.concatenate([down_ref[p], down_ref[p + 1]], axis=1)
        for x_ref, id_ref, acc in ((a_ref, ia_ref, acc_a), (b_ref, ib_ref, acc_b)):
            product = jnp.dot(x_ref[...], wide, preferred_element_type=F32)
            ids = id_ref[...] - (step * per + p)
            total = jnp.where(ids == 0, product[:, :rank], acc[...])
            acc[...] = jnp.where(ids == 1, product[:, rank:], total)

    @pl.when(step == pl.num_programs(0) - 1)
    def _():
        oa_ref[...] = acc_a[...].astype(BF16)
        ob_ref[...] = acc_b[...].astype(BF16)


def inner_products(rows_a, rows_b, ids_a, ids_b, down, after):
    rows, width = rows_a.shape
    owned, _, rank = down.shape
    per = 8
    whole = lambda shape: pl.BlockSpec(shape, lambda i: (0, 0))
    return pl.pallas_call(
        functools.partial(inner_kernel, per),
        grid=(owned // per,),
        in_specs=[
            whole((rows, width)),
            whole((rows, width)),
            whole((rows, 1)),
            whole((rows, 1)),
            pl.BlockSpec((per, width, rank), lambda i: (i, 0, 0)),
        ]
        + [pl.BlockSpec(memory_space=pl.ANY)] * len(after),
        out_specs=[whole((rows, rank)), whole((rows, rank))],
        out_shape=[jax.ShapeDtypeStruct((rows, rank), BF16)] * 2,
        scratch_shapes=[pltpu.VMEM((rows, rank), F32)] * 2,
        compiler_params=pltpu.CompilerParams(vmem_limit_bytes=VMEM_LIMIT),
        cost_estimate=cost(9),
        name="inner_products",
    )(rows_a, rows_b, ids_a, ids_b, down, *after)


def delta_kernel(per, a_ref, b_ref, ia_ref, ib_ref, up_ref, *refs):
    oa_ref, ob_ref, acc_a, acc_b = refs[-4:]
    step = pl.program_id(0)

    @pl.when(step == 0)
    def _():
        acc_a[...] = jnp.zeros_like(acc_a)
        acc_b[...] = jnp.zeros_like(acc_b)

    rank, width = up_ref.shape[1:]
    up = up_ref[...].reshape(per * rank, width)
    for x_ref, id_ref, acc in ((a_ref, ia_ref, acc_a), (b_ref, ib_ref, acc_b)):
        x = x_ref[...]
        ids = id_ref[...]
        wide = jnp.concatenate(
            [jnp.where(ids == step * per + i, x, jnp.zeros_like(x)) for i in range(per)], axis=1
        ).astype(BF16)
        acc[...] += jnp.dot(wide, up, preferred_element_type=F32)

    @pl.when(step == pl.num_programs(0) - 1)
    def _():
        oa_ref[...] = acc_a[...].astype(BF16)
        ob_ref[...] = acc_b[...].astype(BF16)


def adapter_outputs(scaled_a, scaled_b, ids_a, ids_b, up, after):
    rows, rank = scaled_a.shape
    owned, _, width = up.shape
    per = 8
    whole = lambda shape: pl.BlockSpec(shape, lambda i: (0, 0))
    return pl.pallas_call(
        functools.partial(delta_kernel, per),
        grid=(owned // per,),
        in_specs=[
            whole((rows, rank)),
            whole((rows, rank)),
            whole((rows, 1)),
            whole((rows, 1)),
            pl.BlockSpec((per, rank, width), lambda i: (i, 0, 0)),
        ]
        + [pl.BlockSpec(memory_space=pl.ANY)] * len(after),
        out_specs=[whole((rows, width)), whole((rows, width))],
        out_shape=[jax.ShapeDtypeStruct((rows, width), BF16)] * 2,
        scratch_shapes=[pltpu.VMEM((rows, width), F32)] * 2,
        compiler_params=pltpu.CompilerParams(vmem_limit_bytes=VMEM_LIMIT),
        cost_estimate=cost(10),
        name="adapter_outputs",
    )(scaled_a, scaled_b, ids_a, ids_b, up, *after)


def project_kernel(spans, with_delta, where_ref, x_ref, w_ref, *refs):
    n, rows, _ = x_ref.shape
    scratch = refs[-1]
    outs = refs[len(refs) - 1 - 2 * len(spans) : -1]
    step = pl.program_id(0)
    y, z = where_ref[0], where_ref[1]
    blocks = [2 * (z ^ j) + side for side in (y, 1 - y) for j in range(n // 2)]

    @pl.when(step == 0)
    def _():
        for i, block in enumerate(blocks):
            scratch[i * rows : (i + 1) * rows] = x_ref[block]

    result = jnp.dot(scratch[...], w_ref[...], preferred_element_type=F32)
    if with_delta:
        result = result + jnp.concatenate([refs[0][i].astype(F32) for i in blocks], axis=0)
    result = result.astype(BF16)
    for c, (first, count) in enumerate(spans):

        @pl.when((step >= first) & (step < first + count))
        def _():
            for i in range(n):
                o_ref = outs[2 * c + i // (n // 2)]
                o_ref[i % (n // 2)] = result[i * rows : (i + 1) * rows]


def project(y, z, starts, widths, x, weight, delta=None, after=()):
    n, rows, depth = x.shape
    tile = min(512, min(widths))
    spans, table = [], [y, z]
    for start, width in zip(starts, widths):
        spans.append((len(table) - 2, width // tile))
        table += [start // tile + i for i in range(width // tile)]
    steps = len(table) - 2
    ins = [
        pl.BlockSpec((n, rows, depth), lambda i, w: (0, 0, 0)),
        pl.BlockSpec((depth, tile), lambda i, w: (0, w[2 + i])),
    ]
    args = [x, weight]
    if delta is not None:
        ins.append(pl.BlockSpec((n, rows, tile), lambda i, w: (0, 0, i)))
        args.append(delta)

    def out_spec(first, count):
        return pl.BlockSpec(
            (n // 2, rows, tile), lambda i, w: (0, 0, jnp.clip(i - first, 0, count - 1))
        )

    outs = pl.pallas_call(
        functools.partial(project_kernel, spans, delta is not None),
        grid_spec=pltpu.PrefetchScalarGridSpec(
            num_scalar_prefetch=1,
            grid=(steps,),
            in_specs=ins + [pl.BlockSpec(memory_space=pl.ANY)] * len(after),
            out_specs=[out_spec(*span) for span in spans for _ in range(2)],
            scratch_shapes=[pltpu.VMEM((n * rows, depth), BF16)],
        ),
        out_shape=[jax.ShapeDtypeStruct((n // 2, rows, w), BF16) for w in widths for _ in range(2)],
        compiler_params=pltpu.CompilerParams(vmem_limit_bytes=VMEM_LIMIT),
        cost_estimate=cost(1.5 * steps),
        name="project",
    )(jnp.stack(table), *args, *after)
    return outs[::2], outs[1::2]


def add_kernel(near_ref, far_ref, *refs):
    for j, o_ref in enumerate(refs[-near_ref.shape[0] :]):
        o_ref[...] = (near_ref[j].astype(F32) + far_ref[j].astype(F32)).astype(BF16)


def add_sides(near, far, after):
    nz, rows, width = near.shape
    vmem = pl.BlockSpec(memory_space=pltpu.VMEM)
    return pl.pallas_call(
        add_kernel,
        in_specs=[vmem] * 2 + [pl.BlockSpec(memory_space=pl.ANY)] * len(after),
        out_specs=[vmem] * nz,
        out_shape=[jax.ShapeDtypeStruct((rows, width), BF16)] * nz,
        compiler_params=pltpu.CompilerParams(vmem_limit_bytes=VMEM_LIMIT),
        cost_estimate=cost(ADD_US * width * nz / 4096),
        name="add_sides",
    )(near, far, *after)


def finish_kernel(plan, width, place_ref, res_ref, *refs):
    o_ref = refs[-1]
    z, y = place_ref[0], place_ref[1]
    for group, half, terms in plan:
        side = y ^ half
        place = pl.ds(pl.multiple_of(((z ^ group) * 2 + side) * width, width), width)
        total = res_ref[:, place].astype(F32)
        for kind, first in terms:
            if kind == "whole":
                term = refs[first][...]
            elif kind == "half":
                term = refs[first][:, pl.ds(pl.multiple_of(side * width, width), width)]
            else:
                term = jnp.where(side == 0, refs[first[0]][...], refs[first[1]][...])
            total = total + term.astype(F32)
        o_ref[:, place] = total.astype(BF16)


def finish(place, residual, plan, width, arrays):
    rows, features = residual.shape
    vmem = pl.BlockSpec(memory_space=pltpu.VMEM)
    return pl.pallas_call(
        functools.partial(finish_kernel, plan, width),
        in_specs=[pl.BlockSpec(memory_space=pltpu.SMEM), vmem] + [vmem] * len(arrays),
        out_specs=vmem,
        out_shape=jax.ShapeDtypeStruct((rows, features), BF16),
        compiler_params=pltpu.CompilerParams(vmem_limit_bytes=VMEM_LIMIT),
        cost_estimate=cost(2),
        name="finish",
    )(place, residual, *arrays)


def shards(
    n,
    n_dp,
    queries,
    cached_key_rows,
    cached_value_rows,
    fresh_key_value,
    lengths,
    residual,
    output_weight,
    adapter_down,
    adapter_up,
    rank,
    requests,
    row_choice,
):
    nz = n // 2
    me = lax.axis_index("tp").astype(jnp.int32)
    dp = lax.axis_index("dp").astype(jnp.int32)
    z, y = me // 2, me % 2
    rows_dp = queries.shape[1]
    rows = rows_dp // n
    width = queries.shape[2]
    pool_rank = adapter_down.shape[2]
    owned = adapter_down.shape[0]
    fetch = requests.shape[1]

    q = lax.all_to_all(queries[0].reshape(n, rows, width), "tp", 0, 0)
    attended = attend(
        q,
        cached_key_rows[0],
        cached_value_rows[0],
        fresh_key_value[0, :, 0],
        fresh_key_value[0, :, 1],
        lengths[0][:, None],
    )

    choice = row_choice[0]
    lists = requests[0]
    sides = []
    for side in range(2):
        if side == 1:
            choice = permute_xor(choice, "dp", n_dp, 1)
            lists = permute_xor(lists, "dp", n_dp, 1)
        hit = choice[:, None] - owned == jnp.arange(fetch, dtype=jnp.int32)[None, :]
        fetched = jnp.sum(jnp.where(hit, lists[None, :], 0), axis=1)
        slot = jnp.where(choice < owned, (dp ^ side) * owned + choice, fetched)
        local = slot - dp * owned
        mine = (local >= 0) & (local < owned)
        pool = jnp.arange(rank.shape[0], dtype=jnp.int32)
        row_rank = jnp.sum(jnp.where(slot[:, None] == pool[None, :], rank[None, :], 0), axis=1)
        factor = jnp.where(
            (jnp.arange(pool_rank)[None, :] < row_rank[:, None]) & mine[:, None],
            (ADAPTER_SCALE * pool_rank / row_rank.astype(F32))[:, None],
            0.0,
        )
        sides.append((local[:, None], factor))
    (ids_a, factor_a), (ids_b, factor_b) = sides

    x = lax.all_to_all(attended, "tp", 0, 0)
    x_rows = x.reshape(rows_dp, width)
    x_other = permute_xor(x_rows, "dp", n_dp, 1)

    chunks = [(nz - 1, 0, width), (nz - 1, width, width)]
    chunks += [(jz, 0, 2 * width) for jz in reversed(range(1, nz - 1))]
    chunks += [(0, (1 - y) * width, width), (0, y * width, width)]
    count = len(chunks)

    starts = [(z ^ jz) * 2 * width + low for jz, low, _ in chunks]
    widths = [size for _, _, size in chunks]

    def across_y(x):
        return permute_xor(x, "tp", n, 1)

    def along_z(near, far, after):
        total = add_sides(near, far, after)
        return [total[0]] + [permute_xor(total[j], "tp", n, 2 * j) for j in range(1, nz)]

    near, far = project(y, z, starts[:1], widths[:1], x, output_weight)
    more, others = project(y, z, starts[1:-1], widths[1:-1], x, output_weight, after=[near[0]])
    near += more
    far = [across_y(v) for v in far + others]
    inner_a, inner_b = inner_products(x_rows, x_other, ids_a, ids_b, adapter_down, [near[1]])
    received = []
    for i in range(count - 2):
        received.append(along_z(near[i], far[i], received[i - 2][1:] if i >= 2 else []))

    inner = inner_a.astype(F32) + permute_xor(inner_b, "dp", n_dp, 1).astype(F32)
    step = 1
    while step < n:
        inner = inner + permute_xor(inner.astype(BF16), "tp", n, step).astype(F32)
        step *= 2
    inner = inner.astype(BF16)
    inner_other = permute_xor(inner, "dp", n_dp, 1)
    delta_a, delta_b = adapter_outputs(
        (inner.astype(F32) * factor_a).astype(BF16),
        (inner_other.astype(F32) * factor_b).astype(BF16),
        ids_a,
        ids_b,
        adapter_up,
        received[1][1:],
    )
    delta = (delta_a.astype(F32) + permute_xor(delta_b, "dp", n_dp, 1).astype(F32)).astype(BF16)
    delta = delta.reshape(n, rows, width)

    more, others = project(y, z, starts[-1:], widths[-1:], x, output_weight, delta)
    received.append(along_z(more[0], far[-1], received[-2][1:]))
    received.append(along_z(near[-1], across_y(others[0]), received[-2][1:]))

    slots = {(i, j): i * nz + j for i in range(count) for j in range(nz)}
    arrays = [received[i][j] for i in range(count) for j in range(nz)]
    plan = []
    for group in range(nz):
        for half in range(2):
            terms = []
            for j in range(nz):
                jz = group ^ j
                if jz == 0:
                    terms.append(("whole", slots[count - 2 + half, j]))
                elif jz == nz - 1:
                    terms.append(("pick", (slots[0, j], slots[1, j])))
                else:
                    terms.append(("half", slots[nz - jz, j]))
            plan.append((group, half, terms))
    return finish(jnp.stack([z, y]), residual[0], plan, width, arrays)[None]


def solution(mesh):
    return jax.shard_map(
        functools.partial(shards, mesh.shape["tp"], mesh.shape["dp"]),
        mesh=mesh,
        in_specs=(
            P(("groups", "dp"), None, "tp"),
            P(("groups", "dp"), "tp", None, None),
            P(("groups", "dp"), "tp", None, None),
            P(("groups", "dp"), "tp", None, None),
            P(("groups", "dp"), "tp"),
            P(("groups", "dp"), "tp", None),
            P("tp", None),
            P("dp", "tp", None),
            P("dp", None, "tp"),
            P(),
            P(("groups", "dp"), None),
            P(("groups", "dp"), None),
        ),
        out_specs=P(("groups", "dp"), "tp", None),
        check_vma=False,
    )
```

```python
import functools

import jax
import jax.numpy as jnp
from jax import lax
from jax.experimental import pallas as pl
from jax.experimental.pallas import tpu as pltpu
from jax.sharding import PartitionSpec as P

HEADS = 64
KV_HEADS = 8
HEAD_DIM = 128
ADAPTER_SCALE = 0.25
BF16 = jnp.bfloat16
F32 = jnp.float32
ROW_BLOCK = 16
SUB = 8
BATCH = 4
VMEM_LIMIT = 48 * 1024 * 1024


COSTS = {"project": 3.0, "inner": 9.0, "adapter": 10.0, "add": 8.7, "pair": 0.5, "pack": 0.5}
AFTER = {
    "project": {1: [("project", 0)], 2: [("add", 0), ("project", 1)], 3: [("add", 2)]},
    "inner": {0: [("project", 1)]},
    "route": {0: [("sum", 0)], 1: [("z", 0)], 2: [("z", 1)]},
    "sum": {1: [("project", 2)]},
    "delta": {0: [("add", 1)]},
}
LAYOUT = (2,)
CUTS = (1, 2)
HOPS = False


def cost(us):
    return pl.CostEstimate(flops=max(1, int(us * 1.15e9)), bytes_accessed=1, transcendentals=0)


def permute_xor(x, axis, size, k):
    return lax.ppermute(x, axis, [(i, i ^ k) for i in range(size)])


def attend_kernel(n, q_ref, k_ref, v_ref, fk_ref, fv_ref, len_ref, o_ref):
    groups = HEADS // KV_HEADS
    per_src = HEADS // n
    positions = k_ref.shape[1]
    lanes = 2 * positions
    tiles = SUB // 2
    rows = groups * SUB
    row_of = lax.broadcasted_iota(jnp.int32, (rows, lanes), 0) % SUB
    lane_of = lax.broadcasted_iota(jnp.int32, (rows, lanes), 1)
    in_row = (row_of % 2) == (lane_of // positions)
    tile_of = row_of // 2
    scale = HEAD_DIM ** (-0.5)
    parts = [slice(s * SUB, (s + 1) * SUB) for s in range(ROW_BLOCK // SUB)]
    lives = [
        in_row & ((lane_of % positions) < jnp.tile(len_ref[part], (groups, 1))) for part in parts
    ]
    for first in range(0, KV_HEADS, BATCH):
        batch = range(first, first + BATCH)
        scores, owns, values, fresh = [], [], [], []
        for c in batch:
            span = slice(c * HEAD_DIM, (c + 1) * HEAD_DIM)
            heads = [c * groups + h for h in range(groups)]
            q_heads = [
                q_ref[h // per_src, :, (h % per_src) * HEAD_DIM : (h % per_src + 1) * HEAD_DIM].astype(F32)
                for h in heads
            ]
            fresh_key = fk_ref[:, span].astype(F32)
            fresh_value = fv_ref[:, span].astype(F32)
            for part, live in zip(parts, lives):
                q_f32 = jnp.concatenate([q[part] for q in q_heads], axis=0)
                keys = k_ref[part, :, span].reshape(SUB * positions, HEAD_DIM)
                full = lax.dot_general(
                    q_f32.astype(BF16), keys, (((1,), (1,)), ((), ())), preferred_element_type=F32
                )
                score = full[:, :lanes]
                for k in range(1, tiles):
                    score = jnp.where(tile_of == k, full[:, k * lanes : (k + 1) * lanes], score)
                scores.append(jnp.where(live, score * scale, -1e30))
                owns.append(
                    jnp.sum(q_f32 * jnp.tile(fresh_key[part], (groups, 1)), axis=1, keepdims=True) * scale
                )
                fresh.append(jnp.tile(fresh_value[part], (groups, 1)))
                values.append(v_ref[part, :, span].reshape(SUB * positions, HEAD_DIM))
        peaks = [jnp.maximum(jnp.max(s, axis=1, keepdims=True), o) for s, o in zip(scores, owns)]
        weights = [
            jnp.where(live, jnp.exp(s - p), 0.0) for s, p, live in zip(scores, peaks, lives * BATCH)
        ]
        own_weights = [jnp.exp(o - p) for o, p in zip(owns, peaks)]
        totals = [jnp.sum(w, axis=1, keepdims=True) + o for w, o in zip(weights, own_weights)]
        outs = []
        for w, o, t, v, f in zip(weights, own_weights, totals, values, fresh):
            prob = w / t
            prob_new = (o / t).astype(BF16).astype(F32)
            wide = jnp.concatenate([jnp.where(tile_of == k, prob, 0.0) for k in range(tiles)], axis=1)
            outs.append(jnp.dot(wide.astype(BF16), v, preferred_element_type=F32) + prob_new * f)
        for i, c in enumerate(batch):
            pair = outs[i * len(parts) : (i + 1) * len(parts)]
            for g in range(groups):
                h = c * groups + g
                block = jnp.concatenate([o[g * SUB : (g + 1) * SUB] for o in pair], axis=0).astype(BF16)
                o_ref[h // per_src, :, (h % per_src) * HEAD_DIM : (h % per_src + 1) * HEAD_DIM] = block


def attend(q, keys, values, fresh_key, fresh_value, lengths):
    n, rows, width = q.shape
    kv = keys.shape[2]
    positions = keys.shape[1]
    return pl.pallas_call(
        functools.partial(attend_kernel, n),
        grid=(rows // ROW_BLOCK,),
        in_specs=[
            pl.BlockSpec((n, ROW_BLOCK, width), lambda i: (0, i, 0)),
            pl.BlockSpec((ROW_BLOCK, positions, kv), lambda i: (i, 0, 0)),
            pl.BlockSpec((ROW_BLOCK, positions, kv), lambda i: (i, 0, 0)),
            pl.BlockSpec((ROW_BLOCK, kv), lambda i: (i, 0)),
            pl.BlockSpec((ROW_BLOCK, kv), lambda i: (i, 0)),
            pl.BlockSpec((ROW_BLOCK, 1), lambda i: (i, 0)),
        ],
        out_specs=pl.BlockSpec((n, ROW_BLOCK, width), lambda i: (0, i, 0)),
        out_shape=jax.ShapeDtypeStruct((n, rows, width), BF16),
        compiler_params=pltpu.CompilerParams(vmem_limit_bytes=VMEM_LIMIT),
        cost_estimate=cost(9),
        name="attend",
    )(q, keys, values, fresh_key, fresh_value, lengths)


def inner_kernel(per, a_ref, b_ref, ia_ref, ib_ref, down_ref, *refs):
    oa_ref, ob_ref, acc_a, acc_b = refs[-4:]
    step = pl.program_id(0)

    @pl.when(step == 0)
    def _():
        acc_a[...] = jnp.zeros_like(acc_a)
        acc_b[...] = jnp.zeros_like(acc_b)

    rank = down_ref.shape[2]
    for p in range(0, per, 2):
        wide = jnp.concatenate([down_ref[p], down_ref[p + 1]], axis=1)
        for x_ref, id_ref, acc in ((a_ref, ia_ref, acc_a), (b_ref, ib_ref, acc_b)):
            product = jnp.dot(x_ref[...], wide, preferred_element_type=F32)
            ids = id_ref[...] - (step * per + p)
            total = jnp.where(ids == 0, product[:, :rank], acc[...])
            acc[...] = jnp.where(ids == 1, product[:, rank:], total)

    @pl.when(step == pl.num_programs(0) - 1)
    def _():
        oa_ref[...] = acc_a[...].astype(BF16)
        ob_ref[...] = acc_b[...].astype(BF16)


def inner_products(rows_a, rows_b, ids_a, ids_b, down, after):
    rows, width = rows_a.shape
    owned, _, rank = down.shape
    per = 8
    whole = lambda shape: pl.BlockSpec(shape, lambda i: (0, 0))
    return pl.pallas_call(
        functools.partial(inner_kernel, per),
        grid=(owned // per,),
        in_specs=[
            whole((rows, width)),
            whole((rows, width)),
            whole((rows, 1)),
            whole((rows, 1)),
            pl.BlockSpec((per, width, rank), lambda i: (i, 0, 0)),
        ]
        + [pl.BlockSpec(memory_space=pl.ANY)] * len(after),
        out_specs=[whole((rows, rank)), whole((rows, rank))],
        out_shape=[jax.ShapeDtypeStruct((rows, rank), BF16)] * 2,
        scratch_shapes=[pltpu.VMEM((rows, rank), F32)] * 2,
        compiler_params=pltpu.CompilerParams(vmem_limit_bytes=VMEM_LIMIT),
        cost_estimate=cost(COSTS["inner"]),
        name="inner_products",
    )(rows_a, rows_b, ids_a, ids_b, down, *after)


def delta_kernel(per, a_ref, b_ref, ia_ref, ib_ref, up_ref, *refs):
    oa_ref, ob_ref, acc_a, acc_b = refs[-4:]
    step = pl.program_id(0)

    @pl.when(step == 0)
    def _():
        acc_a[...] = jnp.zeros_like(acc_a)
        acc_b[...] = jnp.zeros_like(acc_b)

    rank, width = up_ref.shape[1:]
    up = up_ref[...].reshape(per * rank, width)
    for x_ref, id_ref, acc in ((a_ref, ia_ref, acc_a), (b_ref, ib_ref, acc_b)):
        x = x_ref[...]
        ids = id_ref[...]
        wide = jnp.concatenate(
            [jnp.where(ids == step * per + i, x, jnp.zeros_like(x)) for i in range(per)], axis=1
        ).astype(BF16)
        acc[...] += jnp.dot(wide, up, preferred_element_type=F32)

    @pl.when(step == pl.num_programs(0) - 1)
    def _():
        oa_ref[...] = acc_a[...].astype(BF16)
        ob_ref[...] = acc_b[...].astype(BF16)


def adapter_outputs(scaled_a, scaled_b, ids_a, ids_b, up, after):
    rows, rank = scaled_a.shape
    owned, _, width = up.shape
    per = 8
    whole = lambda shape: pl.BlockSpec(shape, lambda i: (0, 0))
    return pl.pallas_call(
        functools.partial(delta_kernel, per),
        grid=(owned // per,),
        in_specs=[
            whole((rows, rank)),
            whole((rows, rank)),
            whole((rows, 1)),
            whole((rows, 1)),
            pl.BlockSpec((per, rank, width), lambda i: (i, 0, 0)),
        ]
        + [pl.BlockSpec(memory_space=pl.ANY)] * len(after),
        out_specs=[whole((rows, width)), whole((rows, width))],
        out_shape=[jax.ShapeDtypeStruct((rows, width), BF16)] * 2,
        scratch_shapes=[pltpu.VMEM((rows, width), F32)] * 2,
        compiler_params=pltpu.CompilerParams(vmem_limit_bytes=VMEM_LIMIT),
        cost_estimate=cost(COSTS["adapter"]),
        name="adapter_outputs",
    )(scaled_a, scaled_b, ids_a, ids_b, up, *after)


def project_kernel(spans, with_delta, where_ref, x_ref, w_ref, *refs):
    n, rows, _ = x_ref.shape
    scratch = refs[-1]
    outs = refs[len(refs) - 1 - 2 * len(spans) : -1]
    step = pl.program_id(0)
    y, z = where_ref[0], where_ref[1]
    blocks = [2 * (z ^ j) + side for side in (y, 1 - y) for j in range(n // 2)]

    @pl.when(step == 0)
    def _():
        for i, block in enumerate(blocks):
            scratch[i * rows : (i + 1) * rows] = x_ref[block]

    result = jnp.dot(scratch[...], w_ref[...], preferred_element_type=F32)
    if with_delta:
        for d_ref in refs[:2]:
            result = result + jnp.concatenate([d_ref[i].astype(F32) for i in blocks], axis=0)
    result = result.astype(BF16)
    for c, (first, count) in enumerate(spans):

        @pl.when((step >= first) & (step < first + count))
        def _():
            for i in range(n):
                o_ref = outs[2 * c + i // (n // 2)]
                o_ref[i % (n // 2)] = result[i * rows : (i + 1) * rows]


def project(y, z, starts, widths, x, weight, delta=None, after=()):
    n, rows, depth = x.shape
    tile = min(512, min(widths))
    spans, table, first = [], [y, z] + [start // tile for start in starts], 0
    for width in widths:
        spans.append((first, width // tile))
        first += width // tile
    steps = len(table) - 2
    ins = [
        pl.BlockSpec((n, rows, depth), lambda i, w: (0, 0, 0)),
        pl.BlockSpec((depth, tile), lambda i, w: (0, w[2 + i])),
    ]
    args = [x, weight]
    if delta is not None:
        ins += [pl.BlockSpec((n, rows, tile), lambda i, w: (0, 0, i))] * 2
        args += delta

    def out_spec(first, count):
        return pl.BlockSpec(
            (n // 2, rows, tile), lambda i, w: (0, 0, jnp.clip(i - first, 0, count - 1))
        )

    outs = pl.pallas_call(
        functools.partial(project_kernel, spans, delta is not None),
        grid_spec=pltpu.PrefetchScalarGridSpec(
            num_scalar_prefetch=1,
            grid=(steps,),
            in_specs=ins + [pl.BlockSpec(memory_space=pl.ANY)] * len(after),
            out_specs=[out_spec(*span) for span in spans for _ in range(2)],
            scratch_shapes=[pltpu.VMEM((n * rows, depth), BF16)],
        ),
        out_shape=[jax.ShapeDtypeStruct((n // 2, rows, w), BF16) for w in widths for _ in range(2)],
        compiler_params=pltpu.CompilerParams(vmem_limit_bytes=VMEM_LIMIT),
        cost_estimate=cost(COSTS["project"] * steps),
        name="project",
    )(jnp.stack(table), *args, *after)
    return outs[::2], outs[1::2]


def add_pair_kernel(a_ref, b_ref, *refs):
    total = a_ref[...].astype(F32) + b_ref[...].astype(F32)
    refs[-2][...] = total
    refs[-1][...] = total.astype(BF16)


def add_pair(a, b, after):
    vmem = pl.BlockSpec(memory_space=pltpu.VMEM)
    return pl.pallas_call(
        add_pair_kernel,
        in_specs=[vmem] * 2 + [pl.BlockSpec(memory_space=pl.ANY)] * len(after),
        out_specs=[vmem] * 2,
        out_shape=[jax.ShapeDtypeStruct(a.shape, F32), jax.ShapeDtypeStruct(a.shape, BF16)],
        compiler_params=pltpu.CompilerParams(vmem_limit_bytes=VMEM_LIMIT),
        cost_estimate=cost(COSTS["pair"]),
        name="add_pair",
    )(a, b, *after)


def add_kernel(cuts, near_ref, far_ref, *refs):
    first = 0
    for o_ref, cut in zip(refs[-len(cuts) :], cuts):
        o_ref[...] = (near_ref[first : first + cut].astype(F32) + far_ref[first : first + cut].astype(F32)).astype(BF16)
        first += cut


def add_sides(near, far, after):
    nz, rows, width = near.shape
    cuts = [1] * nz
    if HOPS:
        cuts = [1]
        while sum(cuts) < nz:
            cuts.append(sum(cuts))
    vmem = pl.BlockSpec(memory_space=pltpu.VMEM)
    return pl.pallas_call(
        functools.partial(add_kernel, cuts),
        in_specs=[vmem] * 2 + [pl.BlockSpec(memory_space=pl.ANY)] * len(after),
        out_specs=[vmem] * len(cuts),
        out_shape=[jax.ShapeDtypeStruct((cut, rows, width), BF16) for cut in cuts],
        compiler_params=pltpu.CompilerParams(vmem_limit_bytes=VMEM_LIMIT),
        cost_estimate=cost(COSTS["add"] * width * nz / 4096),
        name="add_sides",
    )(near, far, *after)


def pack_kernel(picks, *refs):
    for i, (ref, place) in enumerate(picks):
        refs[-1][i] = refs[ref][place]


def pack(arrays, picks, after):
    rows, width = arrays[0].shape[1:]
    vmem = pl.BlockSpec(memory_space=pltpu.VMEM)
    return pl.pallas_call(
        functools.partial(pack_kernel, picks),
        in_specs=[vmem] * len(arrays) + [pl.BlockSpec(memory_space=pl.ANY)] * len(after),
        out_specs=vmem,
        out_shape=jax.ShapeDtypeStruct((len(picks), rows, width), BF16),
        compiler_params=pltpu.CompilerParams(vmem_limit_bytes=VMEM_LIMIT),
        cost_estimate=cost(COSTS["pack"]),
        name="pack",
    )(*arrays, *after)


def finish_kernel(plan, width, place_ref, res_ref, *refs):
    o_ref = refs[-1]
    z, y = place_ref[0], place_ref[1]
    for group, half, terms in plan:
        side = y ^ half
        place = pl.ds(pl.multiple_of(((z ^ group) * 2 + side) * width, width), width)
        total = res_ref[:, place].astype(F32)
        for term in terms:
            ref, block, k = term[0]
            value = refs[ref][block, :, k * width : (k + 1) * width]
            if len(term) == 2:
                if term[1] == (ref, block, k + 1):
                    first = pl.multiple_of((side + k) * width, width)
                    value = refs[ref][block, :, pl.ds(first, width)]
                else:
                    ref, block, k = term[1]
                    value = jnp.where(side == 0, value, refs[ref][block, :, k * width : (k + 1) * width])
            total = total + value.astype(F32)
        o_ref[:, place] = total.astype(BF16)


def finish(place, residual, plan, width, arrays):
    rows, features = residual.shape
    vmem = pl.BlockSpec(memory_space=pltpu.VMEM)
    return pl.pallas_call(
        functools.partial(finish_kernel, plan, width),
        in_specs=[pl.BlockSpec(memory_space=pltpu.SMEM), vmem] + [vmem] * len(arrays),
        out_specs=vmem,
        out_shape=jax.ShapeDtypeStruct((rows, features), BF16),
        compiler_params=pltpu.CompilerParams(vmem_limit_bytes=VMEM_LIMIT),
        cost_estimate=cost(2),
        name="finish",
    )(place, residual, *arrays)


def shards(
    n,
    n_dp,
    queries,
    cached_key_rows,
    cached_value_rows,
    fresh_key_value,
    lengths,
    residual,
    output_weight,
    adapter_down,
    adapter_up,
    rank,
    requests,
    row_choice,
):
    nz = n // 2
    me = lax.axis_index("tp").astype(jnp.int32)
    dp = lax.axis_index("dp").astype(jnp.int32)
    z, y = me // 2, me % 2
    rows_dp = queries.shape[1]
    rows = rows_dp // n
    width = queries.shape[2]
    pool_rank = adapter_down.shape[2]
    owned = adapter_down.shape[0]
    fetch = requests.shape[1]

    q = lax.all_to_all(queries[0].reshape(n, rows, width), "tp", 0, 0)
    attended = attend(
        q,
        cached_key_rows[0],
        cached_value_rows[0],
        fresh_key_value[0, :, 0],
        fresh_key_value[0, :, 1],
        lengths[0][:, None],
    )

    choice = row_choice[0]
    lists = requests[0]
    sides = []
    for side in range(2):
        if side == 1:
            choice = permute_xor(choice, "dp", n_dp, 1)
            lists = permute_xor(lists, "dp", n_dp, 1)
        hit = choice[:, None] - owned == jnp.arange(fetch, dtype=jnp.int32)[None, :]
        fetched = jnp.sum(jnp.where(hit, lists[None, :], 0), axis=1)
        slot = jnp.where(choice < owned, (dp ^ side) * owned + choice, fetched)
        local = slot - dp * owned
        mine = (local >= 0) & (local < owned)
        pool = jnp.arange(rank.shape[0], dtype=jnp.int32)
        row_rank = jnp.sum(jnp.where(slot[:, None] == pool[None, :], rank[None, :], 0), axis=1)
        factor = jnp.where(
            (jnp.arange(pool_rank)[None, :] < row_rank[:, None]) & mine[:, None],
            (ADAPTER_SCALE * pool_rank / row_rank.astype(F32))[:, None],
            0.0,
        )
        sides.append((local[:, None], factor))
    (ids_a, factor_a), (ids_b, factor_b) = sides

    x = lax.all_to_all(attended, "tp", 0, 0)
    x_rows = x.reshape(rows_dp, width)
    x_other = permute_xor(x_rows, "dp", n_dp, 1)

    blocks = [(jz, b) for jz in reversed(range(1, nz)) for b in range(2)]
    chunks, left = [], list(blocks)
    for size in LAYOUT:
        chunks.append(left[:size])
        left = left[size:]
    while left:
        chunks.append(left[: LAYOUT[-1]])
        left = left[LAYOUT[-1] :]
    chunks += [[(0, 1)], [(0, 0)]]
    count = len(chunks)
    where = {block: (i, k) for i, chunk in enumerate(chunks) for k, block in enumerate(chunk)}
    def start_of(block):
        jz, b = block
        return (z ^ jz) * 2 * width + (b if jz else y ^ b) * width

    def across_y(x):
        return permute_xor(x, "tp", n, 1)

    class Route:
        def __init__(self, near, far, after):
            self.held = list(add_sides(near, far, after))
            self.first = self.held[0]
            self.have = {(0, 0): (0, 0)}
            self.step = 0
            if not HOPS:
                for j in range(1, nz):
                    self.have[j, 0] = (j, 0)
                    self.held[j] = permute_xor(self.held[j], "tp", n, 2 * j)
                return
            for j in range(1, nz):
                bit = j.bit_length() - 1
                self.have[0, j] = (bit + 1, j - (1 << bit))
            self.step = nz // 2
            self.send(self.held[-1], [(0, j) for j in range(nz // 2, nz)])

        def send(self, array, going):
            got = permute_xor(array, "tp", n, 2 * self.step)
            for key in going:
                del self.have[key]
            for i, (source, left) in enumerate(going):
                self.have[source ^ self.step, left ^ self.step] = (len(self.held), i)
            self.held.append(got)
            self.step //= 2

        def forward(self, after):
            going = sorted(key for key in self.have if key[1] & self.step)
            used = sorted({self.have[key][0] for key in going})
            picks = [(used.index(self.have[key][0]), self.have[key][1]) for key in going]
            array = pack([self.held[u] for u in used], picks, after)
            self.send(array, going)
            return array

    made = {}

    def get(name, index=0):
        if (name, index) not in made:
            made[name, index] = RULES[name](index)
        return made[name, index]

    def waits(name, index=0):
        out = []
        for other in AFTER.get(name, {}).get(index, []):
            out += TOKENS[other[0]](*other[1:])
        return out

    bounds = list(zip((0,) + CUTS, CUTS + (count - 1,)))
    bounds = [(a, min(b, count - 1)) for a, b in bounds if a < min(b, count - 1)]

    def rule_project(k):
        if k == len(bounds):
            first, end, delta = count - 1, count, get("delta")
        else:
            first, end, delta = *bounds[k], None
        wide = [len(chunk) * width for chunk in chunks[first:end]]
        tile = min(512, width)
        cols = [start_of(block) + i for chunk in chunks[first:end] for block in chunk for i in range(0, width, tile)]
        near, far = project(y, z, cols, wide, x, output_weight, delta, waits("project", k))
        for i in range(first, end):
            made["near", i] = near[i - first]
            made["far", i] = across_y(far[i - first])
        return near[0]

    def rule_side(name):
        def rule(i):
            k = next((k for k, (a, b) in enumerate(bounds) if a <= i < b), len(bounds))
            get("project", k)
            return made[name, i]

        return rule

    def rule_route(i):
        near = far = i
        if i == count - 2:
            near = count - 1
        elif i == count - 1:
            near = count - 2
        return Route(get("near", near), get("far", far), waits("route", i))

    def rule_inner(_):
        a, b = inner_products(x_rows, x_other, ids_a, ids_b, adapter_down, waits("inner"))
        return a, permute_xor(b, "dp", n_dp, 1)

    def rule_sum(k):
        if k == 0:
            a, b = get("inner")
        else:
            a, b = get("sum", k - 1)
            b = permute_xor(b, "tp", n, 1 << (k - 1))
        return add_pair(a, b, waits("sum", k))

    def rule_delta(_):
        inner, sent = get("sum", n.bit_length() - 1)
        inner_other = permute_xor(sent, "dp", n_dp, 1)
        delta_a, delta_b = adapter_outputs(
            (inner * factor_a).astype(BF16),
            (inner_other.astype(F32) * factor_b).astype(BF16),
            ids_a,
            ids_b,
            adapter_up,
            waits("delta"),
        )
        return [v.reshape(n, rows, width) for v in (delta_a, permute_xor(delta_b, "dp", n_dp, 1))]

    RULES = {
        "project": rule_project,
        "near": rule_side("near"),
        "far": rule_side("far"),
        "route": rule_route,
        "inner": rule_inner,
        "sum": rule_sum,
        "delta": rule_delta,
    }
    TOKENS = {
        "project": lambda i: [get("project", min(i, len(bounds) - 1))],
        "far": lambda i: [get("far", i)],
        "add": lambda i: [get("route", min(i, count - 3)).first],
        "z": lambda i: get("route", min(i, count - 3)).held[1:],
        "inner": lambda: [get("inner")[0]],
        "sum": lambda k: [get("sum", k)[0]],
        "delta": lambda: [get("delta")[0]],
    }
    routes = [get("route", i) for i in range(count)]
    for route in routes:
        while route.step:
            route.forward([])

    arrays, offsets = [], []
    for route in routes:
        offsets.append(len(arrays))
        arrays += route.held
    plan = []
    for group in range(nz):
        for half in range(2):
            terms = []
            for j in range(nz):
                jz = group ^ j
                if jz == 0:
                    i = count - 2 + half
                    held, block = routes[i].have[j, 0]
                    terms.append([(offsets[i] + held, block, 0)])
                    continue
                term = []
                for b in range(2):
                    i, k = where[jz, b]
                    held, block = routes[i].have[j, 0]
                    term.append((offsets[i] + held, block, k))
                terms.append(term)
            plan.append((group, half, terms))
    needed = sorted({t[0] for _, _, terms in plan for term in terms for t in term})
    plan = [
        (g, h, [[(needed.index(r), block, k) for r, block, k in term] for term in terms])
        for g, h, terms in plan
    ]
    return finish(jnp.stack([z, y]), residual[0], plan, width, [arrays[r] for r in needed])[None]


def solution(mesh):
    return jax.shard_map(
        functools.partial(shards, mesh.shape["tp"], mesh.shape["dp"]),
        mesh=mesh,
        in_specs=(
            P(("groups", "dp"), None, "tp"),
            P(("groups", "dp"), "tp", None, None),
            P(("groups", "dp"), "tp", None, None),
            P(("groups", "dp"), "tp", None, None),
            P(("groups", "dp"), "tp"),
            P(("groups", "dp"), "tp", None),
            P("tp", None),
            P("dp", "tp", None),
            P("dp", None, "tp"),
            P(),
            P(("groups", "dp"), None),
            P(("groups", "dp"), None),
        ),
        out_specs=P(("groups", "dp"), "tp", None),
        check_vma=False,
    )
```

```python
import functools

import jax
import jax.numpy as jnp
from jax import lax
from jax.experimental import pallas as pl
from jax.experimental.pallas import tpu as pltpu
from jax.sharding import PartitionSpec as P

HEADS = 64
KV_HEADS = 8
HEAD_DIM = 128
ADAPTER_SCALE = 0.25
BF16 = jnp.bfloat16
F32 = jnp.float32
ROW_BLOCK = 16
SUB = 8
BATCH = 4
VMEM_LIMIT = 48 * 1024 * 1024


COSTS = {"project": 3.0, "inner": 9.0, "adapter": 10.0, "add": 8.7, "pair": 0.5, "pack": 0.5}
AFTER = {
    "project": {1: [("project", 0)], 2: [("add", 0), ("project", 1)], 3: [("add", 2)]},
    "inner": {0: [("project", 1)]},
    "route": {0: [("sum", 0)], 1: [("z", 0)], 2: [("z", 1)]},
    "sum": {1: [("project", 2)], 2: [("add", 1)]},
    "delta": {0: [("add", 1)]},
}
LAYOUT = (2,)
CUTS = (1, 2)
HOPS = False


def cost(us):
    return pl.CostEstimate(flops=max(1, int(us * 1.15e9)), bytes_accessed=1, transcendentals=0)


def permute_xor(x, axis, size, k):
    return lax.ppermute(x, axis, [(i, i ^ k) for i in range(size)])


def attend_kernel(n, q_ref, k_ref, v_ref, fk_ref, fv_ref, len_ref, o_ref):
    groups = HEADS // KV_HEADS
    per_src = HEADS // n
    positions = k_ref.shape[1]
    lanes = 2 * positions
    tiles = SUB // 2
    rows = groups * SUB
    row_of = lax.broadcasted_iota(jnp.int32, (rows, lanes), 0) % SUB
    lane_of = lax.broadcasted_iota(jnp.int32, (rows, lanes), 1)
    in_row = (row_of % 2) == (lane_of // positions)
    tile_of = row_of // 2
    scale = HEAD_DIM ** (-0.5)
    parts = [slice(s * SUB, (s + 1) * SUB) for s in range(ROW_BLOCK // SUB)]
    lives = [
        in_row & ((lane_of % positions) < jnp.tile(len_ref[part], (groups, 1))) for part in parts
    ]
    for first in range(0, KV_HEADS, BATCH):
        batch = range(first, first + BATCH)
        scores, owns, values, fresh = [], [], [], []
        for c in batch:
            span = slice(c * HEAD_DIM, (c + 1) * HEAD_DIM)
            heads = [c * groups + h for h in range(groups)]
            q_heads = [
                q_ref[h // per_src, :, (h % per_src) * HEAD_DIM : (h % per_src + 1) * HEAD_DIM].astype(F32)
                for h in heads
            ]
            fresh_key = fk_ref[:, span].astype(F32)
            fresh_value = fv_ref[:, span].astype(F32)
            for part, live in zip(parts, lives):
                q_f32 = jnp.concatenate([q[part] for q in q_heads], axis=0)
                keys = k_ref[part, :, span].reshape(SUB * positions, HEAD_DIM)
                full = lax.dot_general(
                    q_f32.astype(BF16), keys, (((1,), (1,)), ((), ())), preferred_element_type=F32
                )
                score = full[:, :lanes]
                for k in range(1, tiles):
                    score = jnp.where(tile_of == k, full[:, k * lanes : (k + 1) * lanes], score)
                scores.append(jnp.where(live, score * scale, -1e30))
                owns.append(
                    jnp.sum(q_f32 * jnp.tile(fresh_key[part], (groups, 1)), axis=1, keepdims=True) * scale
                )
                fresh.append(jnp.tile(fresh_value[part], (groups, 1)))
                values.append(v_ref[part, :, span].reshape(SUB * positions, HEAD_DIM))
        peaks = [jnp.maximum(jnp.max(s, axis=1, keepdims=True), o) for s, o in zip(scores, owns)]
        weights = [
            jnp.where(live, jnp.exp(s - p), 0.0) for s, p, live in zip(scores, peaks, lives * BATCH)
        ]
        own_weights = [jnp.exp(o - p) for o, p in zip(owns, peaks)]
        totals = [jnp.sum(w, axis=1, keepdims=True) + o for w, o in zip(weights, own_weights)]
        outs = []
        for w, o, t, v, f in zip(weights, own_weights, totals, values, fresh):
            prob = w / t
            prob_new = (o / t).astype(BF16).astype(F32)
            wide = jnp.concatenate([jnp.where(tile_of == k, prob, 0.0) for k in range(tiles)], axis=1)
            outs.append(jnp.dot(wide.astype(BF16), v, preferred_element_type=F32) + prob_new * f)
        for i, c in enumerate(batch):
            pair = outs[i * len(parts) : (i + 1) * len(parts)]
            for g in range(groups):
                h = c * groups + g
                block = jnp.concatenate([o[g * SUB : (g + 1) * SUB] for o in pair], axis=0).astype(BF16)
                o_ref[h // per_src, :, (h % per_src) * HEAD_DIM : (h % per_src + 1) * HEAD_DIM] = block


def attend(q, keys, values, fresh_key, fresh_value, lengths):
    n, rows, width = q.shape
    kv = keys.shape[2]
    positions = keys.shape[1]
    return pl.pallas_call(
        functools.partial(attend_kernel, n),
        grid=(rows // ROW_BLOCK,),
        in_specs=[
            pl.BlockSpec((n, ROW_BLOCK, width), lambda i: (0, i, 0)),
            pl.BlockSpec((ROW_BLOCK, positions, kv), lambda i: (i, 0, 0)),
            pl.BlockSpec((ROW_BLOCK, positions, kv), lambda i: (i, 0, 0)),
            pl.BlockSpec((ROW_BLOCK, kv), lambda i: (i, 0)),
            pl.BlockSpec((ROW_BLOCK, kv), lambda i: (i, 0)),
            pl.BlockSpec((ROW_BLOCK, 1), lambda i: (i, 0)),
        ],
        out_specs=pl.BlockSpec((n, ROW_BLOCK, width), lambda i: (0, i, 0)),
        out_shape=jax.ShapeDtypeStruct((n, rows, width), BF16),
        compiler_params=pltpu.CompilerParams(vmem_limit_bytes=VMEM_LIMIT),
        cost_estimate=cost(9),
        name="attend",
    )(q, keys, values, fresh_key, fresh_value, lengths)


def inner_kernel(per, a_ref, b_ref, ia_ref, ib_ref, down_ref, *refs):
    oa_ref, ob_ref, acc_a, acc_b = refs[-4:]
    step = pl.program_id(0)

    @pl.when(step == 0)
    def _():
        acc_a[...] = jnp.zeros_like(acc_a)
        acc_b[...] = jnp.zeros_like(acc_b)

    rank = down_ref.shape[2]
    for p in range(0, per, 2):
        wide = jnp.concatenate([down_ref[p], down_ref[p + 1]], axis=1)
        for x_ref, id_ref, acc in ((a_ref, ia_ref, acc_a), (b_ref, ib_ref, acc_b)):
            product = jnp.dot(x_ref[...], wide, preferred_element_type=F32)
            ids = id_ref[...] - (step * per + p)
            total = jnp.where(ids == 0, product[:, :rank], acc[...])
            acc[...] = jnp.where(ids == 1, product[:, rank:], total)

    @pl.when(step == pl.num_programs(0) - 1)
    def _():
        oa_ref[...] = acc_a[...].astype(BF16)
        ob_ref[...] = acc_b[...].astype(BF16)


def inner_products(rows_a, rows_b, ids_a, ids_b, down, after):
    rows, width = rows_a.shape
    owned, _, rank = down.shape
    per = 8
    whole = lambda shape: pl.BlockSpec(shape, lambda i: (0, 0))
    return pl.pallas_call(
        functools.partial(inner_kernel, per),
        grid=(owned // per,),
        in_specs=[
            whole((rows, width)),
            whole((rows, width)),
            whole((rows, 1)),
            whole((rows, 1)),
            pl.BlockSpec((per, width, rank), lambda i: (i, 0, 0)),
        ]
        + [pl.BlockSpec(memory_space=pl.ANY)] * len(after),
        out_specs=[whole((rows, rank)), whole((rows, rank))],
        out_shape=[jax.ShapeDtypeStruct((rows, rank), BF16)] * 2,
        scratch_shapes=[pltpu.VMEM((rows, rank), F32)] * 2,
        compiler_params=pltpu.CompilerParams(vmem_limit_bytes=VMEM_LIMIT),
        cost_estimate=cost(COSTS["inner"]),
        name="inner_products",
    )(rows_a, rows_b, ids_a, ids_b, down, *after)


def delta_kernel(per, a_ref, b_ref, ia_ref, ib_ref, up_ref, *refs):
    oa_ref, ob_ref, acc_a, acc_b = refs[-4:]
    step = pl.program_id(0)

    @pl.when(step == 0)
    def _():
        acc_a[...] = jnp.zeros_like(acc_a)
        acc_b[...] = jnp.zeros_like(acc_b)

    rank, width = up_ref.shape[1:]
    up = up_ref[...].reshape(per * rank, width)
    for x_ref, id_ref, acc in ((a_ref, ia_ref, acc_a), (b_ref, ib_ref, acc_b)):
        x = x_ref[...]
        ids = id_ref[...]
        wide = jnp.concatenate(
            [jnp.where(ids == step * per + i, x, jnp.zeros_like(x)) for i in range(per)], axis=1
        ).astype(BF16)
        acc[...] += jnp.dot(wide, up, preferred_element_type=F32)

    @pl.when(step == pl.num_programs(0) - 1)
    def _():
        oa_ref[...] = acc_a[...].astype(BF16)
        ob_ref[...] = acc_b[...].astype(BF16)


def adapter_outputs(scaled_a, scaled_b, ids_a, ids_b, up, after):
    rows, rank = scaled_a.shape
    owned, _, width = up.shape
    per = 8
    whole = lambda shape: pl.BlockSpec(shape, lambda i: (0, 0))
    return pl.pallas_call(
        functools.partial(delta_kernel, per),
        grid=(owned // per,),
        in_specs=[
            whole((rows, rank)),
            whole((rows, rank)),
            whole((rows, 1)),
            whole((rows, 1)),
            pl.BlockSpec((per, rank, width), lambda i: (i, 0, 0)),
        ]
        + [pl.BlockSpec(memory_space=pl.ANY)] * len(after),
        out_specs=[whole((rows, width)), whole((rows, width))],
        out_shape=[jax.ShapeDtypeStruct((rows, width), BF16)] * 2,
        scratch_shapes=[pltpu.VMEM((rows, width), F32)] * 2,
        compiler_params=pltpu.CompilerParams(vmem_limit_bytes=VMEM_LIMIT),
        cost_estimate=cost(COSTS["adapter"]),
        name="adapter_outputs",
    )(scaled_a, scaled_b, ids_a, ids_b, up, *after)


def project_kernel(spans, with_delta, where_ref, x_ref, w_ref, *refs):
    n, rows, _ = x_ref.shape
    scratch = refs[-1]
    outs = refs[len(refs) - 1 - 2 * len(spans) : -1]
    step = pl.program_id(0)
    y, z = where_ref[0], where_ref[1]
    blocks = [2 * (z ^ j) + side for side in (y, 1 - y) for j in range(n // 2)]

    @pl.when(step == 0)
    def _():
        for i, block in enumerate(blocks):
            scratch[i * rows : (i + 1) * rows] = x_ref[block]

    result = jnp.dot(scratch[...], w_ref[...], preferred_element_type=F32)
    if with_delta:
        for d_ref in refs[:2]:
            result = result + jnp.concatenate([d_ref[i].astype(F32) for i in blocks], axis=0)
    result = result.astype(BF16)
    for c, (first, count) in enumerate(spans):

        @pl.when((step >= first) & (step < first + count))
        def _():
            for i in range(n):
                o_ref = outs[2 * c + i // (n // 2)]
                o_ref[i % (n // 2)] = result[i * rows : (i + 1) * rows]


def project(y, z, starts, widths, x, weight, delta=None, after=()):
    n, rows, depth = x.shape
    tile = min(512, min(widths))
    spans, table, first = [], [y, z] + [start // tile for start in starts], 0
    for width in widths:
        spans.append((first, width // tile))
        first += width // tile
    steps = len(table) - 2
    ins = [
        pl.BlockSpec((n, rows, depth), lambda i, w: (0, 0, 0)),
        pl.BlockSpec((depth, tile), lambda i, w: (0, w[2 + i])),
    ]
    args = [x, weight]
    if delta is not None:
        ins += [pl.BlockSpec((n, rows, tile), lambda i, w: (0, 0, i))] * 2
        args += delta

    def out_spec(first, count):
        return pl.BlockSpec(
            (n // 2, rows, tile), lambda i, w: (0, 0, jnp.clip(i - first, 0, count - 1))
        )

    outs = pl.pallas_call(
        functools.partial(project_kernel, spans, delta is not None),
        grid_spec=pltpu.PrefetchScalarGridSpec(
            num_scalar_prefetch=1,
            grid=(steps,),
            in_specs=ins + [pl.BlockSpec(memory_space=pl.ANY)] * len(after),
            out_specs=[out_spec(*span) for span in spans for _ in range(2)],
            scratch_shapes=[pltpu.VMEM((n * rows, depth), BF16)],
        ),
        out_shape=[jax.ShapeDtypeStruct((n // 2, rows, w), BF16) for w in widths for _ in range(2)],
        compiler_params=pltpu.CompilerParams(vmem_limit_bytes=VMEM_LIMIT),
        cost_estimate=cost(COSTS["project"] * steps),
        name="project",
    )(jnp.stack(table), *args, *after)
    return outs[::2], outs[1::2]


def add_pair_kernel(a_ref, b_ref, *refs):
    total = a_ref[...].astype(F32) + b_ref[...].astype(F32)
    refs[-2][...] = total
    refs[-1][...] = total.astype(BF16)


def add_pair(a, b, after):
    vmem = pl.BlockSpec(memory_space=pltpu.VMEM)
    return pl.pallas_call(
        add_pair_kernel,
        in_specs=[vmem] * 2 + [pl.BlockSpec(memory_space=pl.ANY)] * len(after),
        out_specs=[vmem] * 2,
        out_shape=[jax.ShapeDtypeStruct(a.shape, F32), jax.ShapeDtypeStruct(a.shape, BF16)],
        compiler_params=pltpu.CompilerParams(vmem_limit_bytes=VMEM_LIMIT),
        cost_estimate=cost(COSTS["pair"]),
        name="add_pair",
    )(a, b, *after)


def add_kernel(cuts, near_ref, far_ref, *refs):
    first = 0
    for o_ref, cut in zip(refs[-len(cuts) :], cuts):
        o_ref[...] = (near_ref[first : first + cut].astype(F32) + far_ref[first : first + cut].astype(F32)).astype(BF16)
        first += cut


def add_sides(near, far, after):
    nz, rows, width = near.shape
    cuts = [1] * nz
    if HOPS:
        cuts = [1]
        while sum(cuts) < nz:
            cuts.append(sum(cuts))
    vmem = pl.BlockSpec(memory_space=pltpu.VMEM)
    return pl.pallas_call(
        functools.partial(add_kernel, cuts),
        in_specs=[vmem] * 2 + [pl.BlockSpec(memory_space=pl.ANY)] * len(after),
        out_specs=[vmem] * len(cuts),
        out_shape=[jax.ShapeDtypeStruct((cut, rows, width), BF16) for cut in cuts],
        compiler_params=pltpu.CompilerParams(vmem_limit_bytes=VMEM_LIMIT),
        cost_estimate=cost(COSTS["add"] * width * nz / 4096),
        name="add_sides",
    )(near, far, *after)


def pack_kernel(picks, *refs):
    for i, (ref, place) in enumerate(picks):
        refs[-1][i] = refs[ref][place]


def pack(arrays, picks, after):
    rows, width = arrays[0].shape[1:]
    vmem = pl.BlockSpec(memory_space=pltpu.VMEM)
    return pl.pallas_call(
        functools.partial(pack_kernel, picks),
        in_specs=[vmem] * len(arrays) + [pl.BlockSpec(memory_space=pl.ANY)] * len(after),
        out_specs=vmem,
        out_shape=jax.ShapeDtypeStruct((len(picks), rows, width), BF16),
        compiler_params=pltpu.CompilerParams(vmem_limit_bytes=VMEM_LIMIT),
        cost_estimate=cost(COSTS["pack"]),
        name="pack",
    )(*arrays, *after)


def finish_kernel(plan, width, place_ref, res_ref, *refs):
    o_ref = refs[-1]
    z, y = place_ref[0], place_ref[1]
    for group, half, terms in plan:
        side = y ^ half
        place = pl.ds(pl.multiple_of(((z ^ group) * 2 + side) * width, width), width)
        total = res_ref[:, place].astype(F32)
        for term in terms:
            ref, block, k = term[0]
            value = refs[ref][block, :, k * width : (k + 1) * width]
            if len(term) == 2:
                if term[1] == (ref, block, k + 1):
                    first = pl.multiple_of((side + k) * width, width)
                    value = refs[ref][block, :, pl.ds(first, width)]
                else:
                    ref, block, k = term[1]
                    value = jnp.where(side == 0, value, refs[ref][block, :, k * width : (k + 1) * width])
            total = total + value.astype(F32)
        o_ref[:, place] = total.astype(BF16)


def finish(place, residual, plan, width, arrays):
    rows, features = residual.shape
    vmem = pl.BlockSpec(memory_space=pltpu.VMEM)
    return pl.pallas_call(
        functools.partial(finish_kernel, plan, width),
        in_specs=[pl.BlockSpec(memory_space=pltpu.SMEM), vmem] + [vmem] * len(arrays),
        out_specs=vmem,
        out_shape=jax.ShapeDtypeStruct((rows, features), BF16),
        compiler_params=pltpu.CompilerParams(vmem_limit_bytes=VMEM_LIMIT),
        cost_estimate=cost(2),
        name="finish",
    )(place, residual, *arrays)


def shards(
    n,
    n_dp,
    queries,
    cached_key_rows,
    cached_value_rows,
    fresh_key_value,
    lengths,
    residual,
    output_weight,
    adapter_down,
    adapter_up,
    rank,
    requests,
    row_choice,
):
    nz = n // 2
    me = lax.axis_index("tp").astype(jnp.int32)
    dp = lax.axis_index("dp").astype(jnp.int32)
    z, y = me // 2, me % 2
    rows_dp = queries.shape[1]
    rows = rows_dp // n
    width = queries.shape[2]
    pool_rank = adapter_down.shape[2]
    owned = adapter_down.shape[0]
    fetch = requests.shape[1]

    q = lax.all_to_all(queries[0].reshape(n, rows, width), "tp", 0, 0)
    attended = attend(
        q,
        cached_key_rows[0],
        cached_value_rows[0],
        fresh_key_value[0, :, 0],
        fresh_key_value[0, :, 1],
        lengths[0][:, None],
    )

    choice = row_choice[0]
    lists = requests[0]
    sides = []
    for side in range(2):
        if side == 1:
            choice = permute_xor(choice, "dp", n_dp, 1)
            lists = permute_xor(lists, "dp", n_dp, 1)
        hit = choice[:, None] - owned == jnp.arange(fetch, dtype=jnp.int32)[None, :]
        fetched = jnp.sum(jnp.where(hit, lists[None, :], 0), axis=1)
        slot = jnp.where(choice < owned, (dp ^ side) * owned + choice, fetched)
        local = slot - dp * owned
        mine = (local >= 0) & (local < owned)
        pool = jnp.arange(rank.shape[0], dtype=jnp.int32)
        row_rank = jnp.sum(jnp.where(slot[:, None] == pool[None, :], rank[None, :], 0), axis=1)
        factor = jnp.where(
            (jnp.arange(pool_rank)[None, :] < row_rank[:, None]) & mine[:, None],
            (ADAPTER_SCALE * pool_rank / row_rank.astype(F32))[:, None],
            0.0,
        )
        sides.append((local[:, None], factor))
    (ids_a, factor_a), (ids_b, factor_b) = sides

    x = lax.all_to_all(attended, "tp", 0, 0)
    x_rows = x.reshape(rows_dp, width)
    x_other = permute_xor(x_rows, "dp", n_dp, 1)

    blocks = [(jz, b) for jz in reversed(range(1, nz)) for b in range(2)]
    chunks, left = [], list(blocks)
    for size in LAYOUT:
        chunks.append(left[:size])
        left = left[size:]
    while left:
        chunks.append(left[: LAYOUT[-1]])
        left = left[LAYOUT[-1] :]
    chunks += [[(0, 1)], [(0, 0)]]
    count = len(chunks)
    where = {block: (i, k) for i, chunk in enumerate(chunks) for k, block in enumerate(chunk)}
    def start_of(block):
        jz, b = block
        return (z ^ jz) * 2 * width + (b if jz else y ^ b) * width

    def across_y(x):
        return permute_xor(x, "tp", n, 1)

    class Route:
        def __init__(self, near, far, after):
            self.held = list(add_sides(near, far, after))
            self.first = self.held[0]
            self.have = {(0, 0): (0, 0)}
            self.step = 0
            if not HOPS:
                for j in range(1, nz):
                    self.have[j, 0] = (j, 0)
                    self.held[j] = permute_xor(self.held[j], "tp", n, 2 * j)
                return
            for j in range(1, nz):
                bit = j.bit_length() - 1
                self.have[0, j] = (bit + 1, j - (1 << bit))
            self.step = nz // 2
            self.send(self.held[-1], [(0, j) for j in range(nz // 2, nz)])

        def send(self, array, going):
            got = permute_xor(array, "tp", n, 2 * self.step)
            for key in going:
                del self.have[key]
            for i, (source, left) in enumerate(going):
                self.have[source ^ self.step, left ^ self.step] = (len(self.held), i)
            self.held.append(got)
            self.step //= 2

        def forward(self, after):
            going = sorted(key for key in self.have if key[1] & self.step)
            used = sorted({self.have[key][0] for key in going})
            picks = [(used.index(self.have[key][0]), self.have[key][1]) for key in going]
            array = pack([self.held[u] for u in used], picks, after)
            self.send(array, going)
            return array

    made = {}

    def get(name, index=0):
        if (name, index) not in made:
            made[name, index] = RULES[name](index)
        return made[name, index]

    def waits(name, index=0):
        out = []
        for other in AFTER.get(name, {}).get(index, []):
            out += TOKENS[other[0]](*other[1:])
        return out

    bounds = list(zip((0,) + CUTS, CUTS + (count - 1,)))
    bounds = [(a, min(b, count - 1)) for a, b in bounds if a < min(b, count - 1)]

    def rule_project(k):
        if k == len(bounds):
            first, end, delta = count - 1, count, get("delta")
        else:
            first, end, delta = *bounds[k], None
        wide = [len(chunk) * width for chunk in chunks[first:end]]
        tile = min(512, width)
        cols = [start_of(block) + i for chunk in chunks[first:end] for block in chunk for i in range(0, width, tile)]
        near, far = project(y, z, cols, wide, x, output_weight, delta, waits("project", k))
        for i in range(first, end):
            made["near", i] = near[i - first]
            made["far", i] = across_y(far[i - first])
        return near[0]

    def rule_side(name):
        def rule(i):
            k = next((k for k, (a, b) in enumerate(bounds) if a <= i < b), len(bounds))
            get("project", k)
            return made[name, i]

        return rule

    def rule_route(i):
        near = far = i
        if i == count - 2:
            near = count - 1
        elif i == count - 1:
            near = count - 2
        return Route(get("near", near), get("far", far), waits("route", i))

    def rule_inner(_):
        a, b = inner_products(x_rows, x_other, ids_a, ids_b, adapter_down, waits("inner"))
        return a, permute_xor(b, "dp", n_dp, 1)

    def rule_sum(k):
        if k == 0:
            a, b = get("inner")
        else:
            a, b = get("sum", k - 1)
            b = permute_xor(b, "tp", n, 1 << (k - 1))
        return add_pair(a, b, waits("sum", k))

    def rule_delta(_):
        inner, sent = get("sum", n.bit_length() - 1)
        inner_other = permute_xor(sent, "dp", n_dp, 1)
        delta_a, delta_b = adapter_outputs(
            (inner * factor_a).astype(BF16),
            (inner_other.astype(F32) * factor_b).astype(BF16),
            ids_a,
            ids_b,
            adapter_up,
            waits("delta"),
        )
        return [v.reshape(n, rows, width) for v in (delta_a, permute_xor(delta_b, "dp", n_dp, 1))]

    RULES = {
        "project": rule_project,
        "near": rule_side("near"),
        "far": rule_side("far"),
        "route": rule_route,
        "inner": rule_inner,
        "sum": rule_sum,
        "delta": rule_delta,
    }
    TOKENS = {
        "project": lambda i: [get("project", min(i, len(bounds) - 1))],
        "far": lambda i: [get("far", i)],
        "add": lambda i: [get("route", min(i, count - 3)).first],
        "z": lambda i: get("route", min(i, count - 3)).held[1:],
        "inner": lambda: [get("inner")[0]],
        "sum": lambda k: [get("sum", k)[0]],
        "delta": lambda: [get("delta")[0]],
    }
    routes = [get("route", i) for i in range(count)]
    for route in routes:
        while route.step:
            route.forward([])

    arrays, offsets = [], []
    for route in routes:
        offsets.append(len(arrays))
        arrays += route.held
    plan = []
    for group in range(nz):
        for half in range(2):
            terms = []
            for j in range(nz):
                jz = group ^ j
                if jz == 0:
                    i = count - 2 + half
                    held, block = routes[i].have[j, 0]
                    terms.append([(offsets[i] + held, block, 0)])
                    continue
                term = []
                for b in range(2):
                    i, k = where[jz, b]
                    held, block = routes[i].have[j, 0]
                    term.append((offsets[i] + held, block, k))
                terms.append(term)
            plan.append((group, half, terms))
    needed = sorted({t[0] for _, _, terms in plan for term in terms for t in term})
    plan = [
        (g, h, [[(needed.index(r), block, k) for r, block, k in term] for term in terms])
        for g, h, terms in plan
    ]
    return finish(jnp.stack([z, y]), residual[0], plan, width, [arrays[r] for r in needed])[None]


def solution(mesh):
    return jax.shard_map(
        functools.partial(shards, mesh.shape["tp"], mesh.shape["dp"]),
        mesh=mesh,
        in_specs=(
            P(("groups", "dp"), None, "tp"),
            P(("groups", "dp"), "tp", None, None),
            P(("groups", "dp"), "tp", None, None),
            P(("groups", "dp"), "tp", None, None),
            P(("groups", "dp"), "tp"),
            P(("groups", "dp"), "tp", None),
            P("tp", None),
            P("dp", "tp", None),
            P("dp", None, "tp"),
            P(),
            P(("groups", "dp"), None),
            P(("groups", "dp"), None),
        ),
        out_specs=P(("groups", "dp"), "tp", None),
        check_vma=False,
    )
```
